1024 devices in a mesh: dp: 64 (over x, y, core), fsdp: 16 (over z).
Axes of the slice: x: 4, y: 8, z: 16, core: 2. Of those that a mesh axis runs over, the one named last changes fastest.
Arguments:
- uvqk: bfloat16 [196608, 4096], P(('dp', 'fsdp')), may hold values from -6 to 6
- grad_out: bfloat16 [196608, 1024], P(('dp', 'fsdp')), may hold values from -24 to 24
- w_out: bfloat16 [1024, 1024], P('fsdp'), may hold values from -0.1875 to 0.1875
- kept_segments: int32 [1024, 64], P(('dp', 'fsdp')), may hold values from 0 to 3, never falling along the last dimension, each value on 1 to 32 neighbouring positions
- moved_lengths: int32 [1024, 3], replicated, may hold values from 0 to 128, as said below
- dest_device: int32 [64], replicated, may hold values from 0 to 63, each once
Outputs:
- grad_uvqk: bfloat16 [196608, 4096], P(('dp', 'fsdp'))
- grad_w_out: float32 [1024, 1024], P('fsdp')
The draws below stay inside these ranges and needn't reach their ends.
Inputs may be any that keep to these rules, and one draw needn't show every extreme that they name: `moved_lengths`: the histories of one row sum to at most 128; in every draw some device's block is one history of 128 events.
All inputs are finite; a program needn't handle non-finite values.
Results may differ from the reference program's by a relative error of at most 0.02.
Values may be sent and summed in bfloat16 or wider, within the bound.
No kernel may reach another device: no remote copies, remote signals or barrier semaphores. Data moves between devices by JAX's collectives and lax.ppermute only.
A program may use at most 32 MiB of HBM per device.

```python
import math
import jax
import jax.numpy as jnp
import numpy as np
from jax import lax

D = 1024
HEADS = 4
HIST = 3
KEEP = 64
MOVED = 128
ROWS = 192
N_DP = 64
N_FSDP = 16
DEVICES = 1024


def draw_moved_lengths(key, part):
    key = jax.random.fold_in(key, 5)
    key_live, key_cuts, key_full = jax.random.split(key, 3)
    live = jax.random.randint(key_live, (DEVICES,), MOVED // 2, MOVED + 1).astype(jnp.int32)
    cuts = jnp.sort(jax.random.randint(key_cuts, (DEVICES, HIST - 1), 0, MOVED + 1), axis=1).astype(jnp.int32)
    cuts = jnp.minimum(cuts, live[:, None])
    edges = jnp.concatenate([jnp.zeros((DEVICES, 1), jnp.int32), cuts, live[:, None]], axis=1)
    lengths = (edges[:, 1:] - edges[:, :-1]).astype(jnp.int32)
    full_row = jax.random.randint(key_full, (), 0, DEVICES)
    single = jnp.zeros((HIST,), jnp.int32).at[0].set(MOVED)
    chosen = jnp.arange(DEVICES, dtype=jnp.int32)[:, None] == full_row
    return jnp.where(chosen, single[None, :], lengths).astype(jnp.int32)


def with_spikes(drawn, stream_key, source, target, shards_of, factor):
    def block_of(dim):
        return (jnp.arange(drawn.shape[dim]) // (drawn.shape[dim] // shards_of)).reshape((-1,) + (1,) * (drawn.ndim - 1 - dim))

    first = jax.random.permutation(stream_key, shards_of)[block_of(target)]
    far = (block_of(target) + shards_of // 2) % shards_of
    return jnp.where((block_of(source) == first) | (block_of(source) == far), factor * drawn, drawn)


def steps_of(stream_key, extent, cuts, least, top_value):
    loudness = 1.0
    for dim, parts in cuts:
        steps = jax.random.uniform(jax.random.fold_in(jax.random.fold_in(stream_key, 6), dim), (parts,), jnp.float32, least / len(cuts), top_value / len(cuts))
        loudness = loudness * jnp.repeat(jnp.exp(steps), extent[dim] // parts).reshape((-1,) + (1,) * (len(extent) - 1 - dim))
    return loudness


def profile(count, total, bound, lean):
    weights = [(1 << 20) // math.isqrt(rank ** lean) + 1 for rank in range(2, count + 1)]
    spare, holding = total - bound - (count - 1), [1] * (count - 1)
    while spare > 0:
        free = [i for i in range(count - 1) if holding[i] < bound]
        whole, left = sum([weights[i] for i in free]), spare
        for i in free:
            extra = min(bound - holding[i], max(1, left * weights[i] // whole), spare)
            holding[i] = holding[i] + extra
            spare = spare - extra
    return np.array([bound] + holding)


def ragged(own_key, count, total, limit, slope):
    if count == 2:
        one = jax.random.randint(own_key, (), max(1, total - limit), min(limit, total - 1) + 1)
        return jnp.stack([one, total - one])
    sizes = jnp.asarray(profile(count, total, limit, slope), jnp.int32)
    twos = (count - 1) // 2
    donor, sink = sizes[1:1 + 2 * twos:2], sizes[2:2 + 2 * twos:2]
    slack = jnp.minimum(donor - 1, limit - sink)
    shifted = jax.random.randint(jax.random.fold_in(own_key, 1), (twos,), 0, 1 << 20) % (slack + 1)
    sizes = sizes.at[1:1 + 2 * twos:2].set(donor - shifted).at[2:2 + 2 * twos:2].set(sink + shifted)
    return sizes[jax.random.permutation(jax.random.fold_in(own_key, 2), count)]


def noise(stream_key, extent, scale, reach, shards=(), kind=jnp.bfloat16):
    result = scale * jax.random.normal(stream_key, extent, jnp.float32)
    if shards:
        result = result * steps_of(stream_key, extent, shards, -0.22, 0.18)
    return jnp.clip(result, -reach, reach).astype(kind)


def heavy_noise(stream_key, dims, spread, bound, cuts, heavy, held_as=jnp.bfloat16):
    entries = spread * jax.random.normal(stream_key, dims, jnp.float32)
    if cuts:
        entries = entries * steps_of(stream_key, dims, cuts, -0.22, 0.18)
    return jnp.clip(with_spikes(entries, jax.random.fold_in(stream_key, 3), *heavy), -bound, bound).astype(held_as)


def setup_inputs(seed: int = 0) -> dict:
    keys = jax.random.split(jax.random.key(seed), 7)
    return {
        "uvqk": noise(keys[0], (DEVICES * ROWS, 4 * D), 1.0, 6.0, ((0, 1024),)),
        "grad_out": heavy_noise(keys[1], (DEVICES * ROWS, D), 1.0, 24.0, ((0, 1024),), (0, 1, 1024, 6.0)),
        "w_out": noise(keys[2], (D, D), D ** -0.5, 0.1875, ((0, 16),)),
        "kept_segments": jax.vmap(lambda own: jnp.searchsorted(jnp.cumsum(ragged(own, 4, KEEP, KEEP // 2, 2)), jnp.arange(KEEP), side="right"))(jax.random.split(keys[3], DEVICES)).reshape((DEVICES, KEEP)).astype(jnp.int32),
        "moved_lengths": draw_moved_lengths(jax.random.fold_in(keys[6], 71), 0),
        "dest_device": jax.random.permutation(keys[5], N_DP).astype(jnp.int32),
    }


EPS = 1e-05

def rounded(values):
    return lax.optimization_barrier(values.astype(jnp.bfloat16)).astype(jnp.float32)

def silu_slope(scores):
    sigma = jax.nn.sigmoid(scores)
    return sigma * (1.0 + scores * (1.0 - sigma))

def attend(gate, others, segments):
    length = gate.shape[0]
    head_dim = D // HEADS
    score_scale = 1.0 / math.sqrt(head_dim)
    split_rest = others.astype(jnp.float32).reshape(length, 3, HEADS, head_dim)
    values = split_rest[:, 0]
    queries = split_rest[:, 1]
    key_rows = split_rest[:, 2]
    positions = jnp.arange(length, dtype=jnp.int32)
    same_history = segments[:, None] == segments[None, :]
    allowed = same_history & (positions[None, :] <= positions[:, None]) & (segments >= 0)[:, None]
    counts = lax.optimization_barrier(jnp.sum(same_history.astype(jnp.float32), axis=1))
    scores = jnp.einsum('ihe,jhe->hij', queries, key_rows) * score_scale
    weights = rounded(jnp.where(allowed[None], jax.nn.silu(scores), 0.0) / counts[None, :, None])
    mixed = jnp.einsum('hij,jhe->ihe', weights, values).reshape(length, D)
    centered = mixed - lax.optimization_barrier(jnp.mean(mixed, axis=1, keepdims=True))
    inverse = lax.rsqrt(lax.optimization_barrier(jnp.mean(centered * centered, axis=1, keepdims=True)) + EPS)
    normed = centered * inverse
    gate_float = gate.astype(jnp.float32)
    output_rows = (normed * gate_float).astype(jnp.bfloat16)
    return (scores, allowed, counts, weights, normed, inverse, gate_float, values, queries, key_rows, output_rows)

def attend_back(stored, grad_y):
    scores, allowed, counts, weights, normed, inverse, gate_float, values, queries, key_rows, output_rows = stored
    length = normed.shape[0]
    head_dim = D // HEADS
    score_scale = 1.0 / math.sqrt(head_dim)
    grad_gate = (grad_y * normed).astype(jnp.bfloat16)
    grad_normed = grad_y * gate_float
    grad_mixed = inverse * (grad_normed - lax.optimization_barrier(jnp.mean(grad_normed, axis=1, keepdims=True)) - normed * lax.optimization_barrier(jnp.mean(grad_normed * normed, axis=1, keepdims=True)))
    grad_mixed = rounded(grad_mixed).reshape(length, HEADS, head_dim)
    grad_weights = jnp.einsum('ihe,jhe->hij', grad_mixed, values)
    grad_values = jnp.einsum('hij,ihe->jhe', weights, grad_mixed).astype(jnp.bfloat16)
    grad_scores = jnp.where(allowed[None], grad_weights * silu_slope(scores), 0.0) * score_scale / counts[None, :, None]
    grad_scores = rounded(grad_scores)
    grad_queries = jnp.einsum('hij,jhe->ihe', grad_scores, key_rows).astype(jnp.bfloat16)
    grad_keys = jnp.einsum('hij,ihe->jhe', grad_scores, queries).astype(jnp.bfloat16)
    return jnp.concatenate([grad_gate, grad_values.reshape(length, D), grad_queries.reshape(length, D), grad_keys.reshape(length, D)], axis=1)

def reference(uvqk, grad_out, w_out, kept_segments, moved_lengths, dest_device):
    row_blocks = uvqk.reshape(N_DP, N_FSDP, KEEP + MOVED, 4 * D)
    grad_blocks = grad_out.reshape(N_DP, N_FSDP, KEEP + MOVED, D)
    forward_map = dest_device.astype(jnp.int32)
    indices = jnp.arange(N_DP, dtype=jnp.int32)
    source_of = lax.optimization_barrier(jnp.sum(jnp.where(forward_map[None, :] == indices[:, None], indices[None, :], 0), axis=1)).astype(jnp.int32)
    received_in = row_blocks[source_of][:, :, KEEP:]
    received_grad = grad_blocks[source_of][:, :, KEEP:]
    lengths = moved_lengths.astype(jnp.int32).reshape(N_DP, N_FSDP, HIST)[source_of]
    ends = jnp.cumsum(lengths, axis=-1)
    places = jnp.arange(MOVED, dtype=jnp.int32)
    seg_ids = lax.optimization_barrier(jnp.sum((places[:, None] >= ends[:, :, None, :]).astype(jnp.int32), axis=-1))
    recv_segments = jnp.where(seg_ids == HIST, -1, seg_ids).astype(jnp.int32)
    packed = (row_blocks[:, :, :KEEP].reshape(DEVICES, KEEP, 4 * D), grad_blocks[:, :, :KEEP].reshape(DEVICES, KEEP, D), received_in.reshape(DEVICES, MOVED, 4 * D), received_grad.reshape(DEVICES, MOVED, D), kept_segments.astype(jnp.int32), recv_segments.reshape(DEVICES, MOVED))

    def device_step(accumulated, packed_one):
        kept_in, kept_grad, recv_in, recv_grad, kept_seg, recv_seg = packed_one
        stored_kept = attend(kept_in[:, :D], kept_in[:, D:], kept_seg)
        stored_recv = attend(recv_in[:, :D], recv_in[:, D:], recv_seg)
        grads_all = jnp.concatenate([kept_grad, recv_grad], axis=0)
        outputs_all = jnp.concatenate([stored_kept[-1], stored_recv[-1]], axis=0)
        grad_outputs = jnp.dot(grads_all, w_out, preferred_element_type=jnp.float32)
        device_term = lax.dot_general(grads_all, outputs_all, (((0,), (0,)), ((), ())), preferred_element_type=jnp.float32)
        accumulated = accumulated + rounded(device_term)
        kept_back = attend_back(stored_kept, grad_outputs[:KEEP])
        recv_back = attend_back(stored_recv, grad_outputs[KEEP:])
        return (accumulated, jnp.concatenate([kept_back, recv_back], axis=0))
    accumulated, backs = lax.scan(device_step, jnp.zeros((D, D), jnp.float32), packed)
    return (backs.reshape(DEVICES * (KEEP + MOVED), 4 * D), accumulated / DEVICES)
```

```python
import functools
import math

import jax
import jax.numpy as jnp
from jax import lax
from jax.experimental import pallas as pl
from jax.experimental.pallas import tpu as pltpu
from jax.sharding import Mesh
from jax.sharding import PartitionSpec as P

HEADS = 4
EPS = 1e-05
GROUP_ROWS = 16
BF16 = jnp.bfloat16
F32 = jnp.float32
DP = ("x", "y", "core")


def dot(a, b, dims):
    return lax.dot_general(a, b, (dims, ((), ())), preferred_element_type=F32)


def segments_of(ends, shape, dim):
    places = lax.broadcasted_iota(jnp.int32, shape, dim)
    passed = jnp.zeros(shape, jnp.int32)
    for end in ends:
        passed = passed + (places >= end).astype(jnp.int32)
    return jnp.where(passed == len(ends), -1, passed)


def masks(seg_column, seg_row):
    length = seg_column.shape[0]
    square = (length, length)
    same = seg_column == seg_row
    earlier = lax.broadcasted_iota(jnp.int32, square, 1) <= lax.broadcasted_iota(jnp.int32, square, 0)
    allowed = same & earlier & (seg_column >= 0)
    counts = jnp.sum(same.astype(F32), axis=1, keepdims=True)
    return allowed, counts


def forward(values, queries, key_rows, allowed, counts):
    width = values.shape[1]
    head_dim = width // HEADS
    scale = 1.0 / math.sqrt(head_dim)
    scores, sigmas, weights, mixed = [], [], [], []
    for h in range(HEADS):
        cols = slice(h * head_dim, (h + 1) * head_dim)
        s = dot(queries[:, cols], key_rows[:, cols], ((1,), (1,))) * scale
        sigma = jax.nn.sigmoid(s)
        w = (jnp.where(allowed, s * sigma, 0.0) / counts).astype(BF16)
        scores.append(s)
        sigmas.append(sigma)
        weights.append(w)
        mixed.append(dot(w, values[:, cols], ((1,), (0,))))
    mixed = jnp.concatenate(mixed, axis=1)
    centered = mixed - jnp.mean(mixed, axis=1, keepdims=True)
    inverse = lax.rsqrt(jnp.mean(centered * centered, axis=1, keepdims=True) + EPS)
    return scores, sigmas, weights, centered * inverse, inverse


def backward(gate, values, queries, key_rows, grad_y, allowed, counts, put):
    width = values.shape[1]
    head_dim = width // HEADS
    scale = 1.0 / math.sqrt(head_dim)
    scores, sigmas, weights, normed, inverse = forward(values, queries, key_rows, allowed, counts)
    put(0, slice(0, width), grad_y * normed)
    grad_normed = grad_y * gate.astype(F32)
    grad_mixed = inverse * (
        grad_normed
        - jnp.mean(grad_normed, axis=1, keepdims=True)
        - normed * jnp.mean(grad_normed * normed, axis=1, keepdims=True)
    )
    grad_mixed = grad_mixed.astype(BF16)
    factor = scale / counts
    for h in range(HEADS):
        cols = slice(h * head_dim, (h + 1) * head_dim)
        s, sigma = scores[h], sigmas[h]
        grad_weights = dot(grad_mixed[:, cols], values[:, cols], ((1,), (1,)))
        put(1, cols, dot(weights[h], grad_mixed[:, cols], ((0,), (0,))))
        slope = sigma * (1.0 + s * (1.0 - sigma))
        grad_scores = (jnp.where(allowed, grad_weights * slope, 0.0) * factor).astype(BF16)
        put(2, cols, dot(grad_scores, key_rows[:, cols], ((1,), (0,))))
        put(3, cols, dot(grad_scores, queries[:, cols], ((0,), (0,))))


def shares(row_groups, col_groups, share_cols):
    for r in range(row_groups):
        for c in range(col_groups):
            yield r * col_groups + c, r * GROUP_ROWS, c * share_cols


def pack_kernel(keep, x_ref, g_ref, out_ref):
    width, joint = x_ref.shape[1], x_ref.shape[1] + g_ref.shape[1]
    row_groups = (x_ref.shape[0] - keep) // GROUP_ROWS
    share_cols = out_ref.shape[2]
    for share, row, start in shares(row_groups, joint // share_cols, share_cols):
        rows = pl.ds(keep + row, GROUP_ROWS)
        split = min(max(width - start, 0), share_cols)
        if split > 0:
            out_ref[share, :, pl.ds(0, split)] = x_ref[rows, pl.ds(start, split)]
        if split < share_cols:
            out_ref[share, :, pl.ds(split, share_cols - split)] = g_ref[
                rows, pl.ds(start + split - width, share_cols - split)
            ]


def term_kernel(keep, lengths_ref, x_ref, g_ref, seg_col_ref, seg_row_ref, term_ref, y_ref):
    width = g_ref.shape[1]
    rows_all = x_ref.shape[0]

    def rows_of(rows, allowed, counts):
        values, queries, key_rows = (x_ref[rows, pl.ds((1 + i) * width, width)] for i in range(3))
        normed = forward(values, queries, key_rows, allowed, counts)[3]
        y_ref[rows, :] = (normed * x_ref[rows, pl.ds(0, width)].astype(F32)).astype(BF16)

    moved = rows_all - keep
    total, ends = 0, []
    for i in range(lengths_ref.shape[1]):
        total = total + lengths_ref[0, i]
        ends.append(total)
    rows_of(pl.ds(keep, moved), *masks(segments_of(ends, (moved, 1), 0), segments_of(ends, (1, moved), 1)))
    rows_of(pl.ds(0, keep), *masks(seg_col_ref[...], seg_row_ref[...]))
    blocks, _, block_cols = term_ref.shape
    joined = max(1, 256 // block_cols)
    for b in range(0, blocks, joined):
        found = dot(g_ref[...], y_ref[:, pl.ds(b * block_cols, joined * block_cols)], ((0,), (0,)))
        for i in range(joined):
            term_ref[b + i] = found[:, i * block_cols : (i + 1) * block_cols].astype(BF16)


def back_kernel(keep, lengths_ref, x_ref, g_ref, came_ref, w_ref, seg_col_ref, seg_row_ref, out_ref, block_ref):
    width = g_ref.shape[1]
    moved, joint = block_ref.shape
    share_cols = came_ref.shape[2]
    for share, row, start in shares(moved // GROUP_ROWS, joint // share_cols, share_cols):
        block_ref[pl.ds(row, GROUP_ROWS), pl.ds(start, share_cols)] = came_ref[share]

    def put_in(rows):
        def put(part, cols, found):
            out_ref[rows, pl.ds(part * width + cols.start, cols.stop - cols.start)] = found.astype(BF16)

        return put

    total, ends = 0, []
    for i in range(lengths_ref.shape[1]):
        total = total + lengths_ref[0, i]
        ends.append(total)
    kept_grad_y = dot(g_ref[pl.ds(0, keep), :], w_ref[...], ((1,), (0,)))
    parts = [x_ref[pl.ds(0, keep), pl.ds(i * width, width)] for i in range(4)]
    backward(*parts, kept_grad_y, *masks(seg_col_ref[...], seg_row_ref[...]), put_in(pl.ds(0, keep)))
    *parts, grads = [block_ref[:, pl.ds(i * width, width)] for i in range(5)]
    grad_y = dot(grads, w_ref[...], ((1,), (0,)))
    backward(
        *parts,
        grad_y,
        *masks(segments_of(ends, (moved, 1), 0), segments_of(ends, (1, moved), 1)),
        put_in(pl.ds(keep, moved)),
    )


VMEM = pl.BlockSpec(memory_space=pltpu.VMEM)
SMEM = pl.BlockSpec(memory_space=pltpu.SMEM)
PARAMS = pltpu.CompilerParams(vmem_limit_bytes=40 * 2**20)


def cost(flops, nbytes):
    return pl.CostEstimate(flops=flops, bytes_accessed=nbytes, transcendentals=0)


def permuted(value, axis, target):
    size = lax.axis_size(axis)
    return lax.ppermute(value, axis, [(i, target(i)) for i in range(size)])


def pick(value, index, dim=0):
    return lax.dynamic_index_in_dim(value, index, dim, keepdims=False)


def added(*values):
    return functools.reduce(jnp.add, [value.astype(F32) for value in values])


def scatter_sum(value, axis):
    size, me = lax.axis_size(axis), lax.axis_index(axis)
    came = [
        permuted(pick(value, (me + step) & (size - 1)), axis, lambda i, step=step: (i + step) % size)
        for step in range(1, size)
    ]
    return added(pick(value, me), *came).astype(BF16)


def halving_sum(value, axis):
    size, me = lax.axis_size(axis), lax.axis_index(axis)
    steps = size.bit_length() - 1
    for step in range(steps):
        pairs = value.reshape((value.shape[0] // 2, 2) + value.shape[1:])
        mine = (me >> step) & 1
        came = permuted(pick(pairs, 1 - mine, 1), axis, lambda i, step=step: i ^ (1 << step))
        value = added(pick(pairs, mine, 1), came)
        if step < steps - 1:
            value = value.astype(BF16)
    return value[0]


def doubling_sum(value, axis):
    for step in range(lax.axis_size(axis).bit_length() - 1):
        value = value + permuted(value, axis, lambda i, step=step: i ^ (1 << step))
    return value


def doubling_gather(value, axis):
    me = lax.axis_index(axis)
    for step in range(lax.axis_size(axis).bit_length() - 1):
        came = permuted(value, axis, lambda i, step=step: i ^ (1 << step))
        low = ((me >> step) & 1) == 0
        value = jnp.concatenate([jnp.where(low, value, came), jnp.where(low, came, value)], axis=1)
    return value


def exchange(value):
    return lax.all_to_all(value, DP, split_axis=0, concat_axis=0, tiled=True)


def local(uvqk, grad_out, w_out, kept_segments, moved_lengths, dest_device):
    keep = kept_segments.shape[1]
    rows, width = grad_out.shape
    moved = rows - keep
    n_x, n_y, n_core, n_z = (lax.axis_size(a) for a in ("x", "y", "core", "z"))
    groups = n_x * n_y * n_core
    dp_index, z_index = lax.axis_index(DP), lax.axis_index("z")
    indices = jnp.arange(groups, dtype=jnp.int32)
    source_of = jnp.sum(jnp.where(dest_device[None, :] == indices[:, None], indices[None, :], 0), axis=1)
    own_source = jnp.sum(jnp.where(dest_device == dp_index, indices, 0))
    own_lengths = lax.dynamic_slice_in_dim(moved_lengths, dp_index * n_z + z_index, 1, 0)
    recv_lengths = lax.dynamic_slice_in_dim(moved_lengths, own_source * n_z + z_index, 1, 0)
    seg_col, seg_row = kept_segments.reshape(keep, 1), kept_segments

    w_all = lax.all_gather(w_out, "z", axis=0, tiled=True)
    share_cols = 5 * width * (moved // GROUP_ROWS) // groups
    block = pl.pallas_call(
        functools.partial(pack_kernel, keep),
        out_shape=jax.ShapeDtypeStruct((groups, GROUP_ROWS, share_cols), BF16),
        in_specs=[VMEM, VMEM],
        out_specs=VMEM,
        compiler_params=PARAMS,
        cost_estimate=cost(0, 10 * moved * 5 * width),
        name="pack",
    )(uvqk, grad_out)
    uvqk, grad_out, block = lax.optimization_barrier((uvqk, grad_out, block))
    block = exchange(block)

    blocks = n_core * n_x
    block_cols = width // blocks
    term = pl.pallas_call(
        functools.partial(term_kernel, keep),
        out_shape=jax.ShapeDtypeStruct((blocks, width, block_cols), BF16),
        in_specs=[SMEM, VMEM, VMEM, VMEM, VMEM],
        out_specs=VMEM,
        scratch_shapes=[pltpu.VMEM((rows, width), BF16)],
        compiler_params=PARAMS,
        cost_estimate=cost(4 * rows * width * width, 8 * width * width),
        name="term",
    )(own_lengths, uvqk, grad_out, seg_col, seg_row)
    part = scatter_sum(term.reshape(n_core, n_x, width, block_cols), "core")
    part = scatter_sum(part, "x")
    own_rows = width // n_z
    part = halving_sum(part.reshape(n_z, own_rows, block_cols), "z")
    part = doubling_sum(part, "y") * (1.0 / (groups * n_z))
    grad_weight = doubling_gather(doubling_gather(part, "x"), "core")

    block = exchange(block[source_of])
    grad_rows = pl.pallas_call(
        functools.partial(back_kernel, keep),
        out_shape=jax.ShapeDtypeStruct(uvqk.shape, BF16),
        in_specs=[SMEM] + [VMEM] * 6,
        out_specs=VMEM,
        scratch_shapes=[pltpu.VMEM((moved, 5 * width), BF16)],
        compiler_params=PARAMS,
        cost_estimate=cost(8 * rows * width * width, 8 * width * width),
        name="back",
    )(recv_lengths, uvqk, grad_out, block, w_all, seg_col, seg_row)
    return grad_rows, grad_weight


def fine_mesh(mesh):
    n_dp, n_z = mesh.devices.shape
    n_core = 2
    n_x = min(4, n_dp // 4)
    shape = (n_x, n_dp // (n_x * n_core), n_core, n_z)
    return Mesh(mesh.devices.reshape(shape), ("x", "y", "core", "z"))


def solution(mesh):
    everyone = P(("x", "y", "core", "z"), None)
    placed = (everyone, everyone, P("z", None), everyone, P(), P())
    return jax.shard_map(
        local,
        mesh=fine_mesh(mesh),
        in_specs=placed,
        out_specs=(everyone, P("z", None)),
        check_vma=False,
    )
```

```python
import functools
import math

import jax
import jax.numpy as jnp
from jax import lax
from jax.experimental import pallas as pl
from jax.experimental.pallas import tpu as pltpu
from jax.sharding import Mesh
from jax.sharding import PartitionSpec as P

HEADS = 4
EPS = 1e-05
GROUP_ROWS = 16
BF16 = jnp.bfloat16
F32 = jnp.float32
DP = ("x", "y", "core")


def dot(a, b, dims):
    return lax.dot_general(a, b, (dims, ((), ())), preferred_element_type=F32)


def segments_of(ends, shape, dim):
    places = lax.broadcasted_iota(jnp.int32, shape, dim)
    passed = jnp.zeros(shape, jnp.int32)
    for end in ends:
        passed = passed + (places >= end).astype(jnp.int32)
    return jnp.where(passed == len(ends), -1, passed)


def masks(seg_column, seg_row):
    length = seg_column.shape[0]
    square = (length, length)
    same = seg_column == seg_row
    earlier = lax.broadcasted_iota(jnp.int32, square, 1) <= lax.broadcasted_iota(jnp.int32, square, 0)
    allowed = same & earlier & (seg_column >= 0)
    counts = jnp.sum(same.astype(F32), axis=1, keepdims=True)
    return allowed, counts


def forward(values, queries, key_rows, allowed, counts):
    width = values.shape[1]
    head_dim = width // HEADS
    scale = 1.0 / math.sqrt(head_dim)
    scores, sigmas, weights, mixed = [], [], [], []
    for h in range(HEADS):
        cols = slice(h * head_dim, (h + 1) * head_dim)
        s = dot(queries[:, cols], key_rows[:, cols], ((1,), (1,))) * scale
        sigma = jax.nn.sigmoid(s)
        w = (jnp.where(allowed, s * sigma, 0.0) / counts).astype(BF16)
        scores.append(s)
        sigmas.append(sigma)
        weights.append(w)
        mixed.append(dot(w, values[:, cols], ((1,), (0,))))
    mixed = jnp.concatenate(mixed, axis=1)
    centered = mixed - jnp.mean(mixed, axis=1, keepdims=True)
    inverse = lax.rsqrt(jnp.mean(centered * centered, axis=1, keepdims=True) + EPS)
    return scores, sigmas, weights, centered * inverse, inverse


def backward(gate, values, queries, key_rows, grad_y, allowed, counts, put):
    width = values.shape[1]
    head_dim = width // HEADS
    scale = 1.0 / math.sqrt(head_dim)
    scores, sigmas, weights, normed, inverse = forward(values, queries, key_rows, allowed, counts)
    put(0, slice(0, width), grad_y * normed)
    grad_normed = grad_y * gate.astype(F32)
    grad_mixed = inverse * (
        grad_normed
        - jnp.mean(grad_normed, axis=1, keepdims=True)
        - normed * jnp.mean(grad_normed * normed, axis=1, keepdims=True)
    )
    grad_mixed = grad_mixed.astype(BF16)
    factor = scale / counts
    for h in range(HEADS):
        cols = slice(h * head_dim, (h + 1) * head_dim)
        s, sigma = scores[h], sigmas[h]
        grad_weights = dot(grad_mixed[:, cols], values[:, cols], ((1,), (1,)))
        put(1, cols, dot(weights[h], grad_mixed[:, cols], ((0,), (0,))))
        slope = sigma * (1.0 + s * (1.0 - sigma))
        grad_scores = (jnp.where(allowed, grad_weights * slope, 0.0) * factor).astype(BF16)
        put(2, cols, dot(grad_scores, key_rows[:, cols], ((1,), (0,))))
        put(3, cols, dot(grad_scores, queries[:, cols], ((0,), (0,))))


def shares(row_groups, col_groups, share_cols):
    for r in range(row_groups):
        for c in range(col_groups):
            yield r * col_groups + c, r * GROUP_ROWS, c * share_cols


def pack_kernel(keep, x_ref, g_ref, out_ref):
    width, joint = x_ref.shape[1], x_ref.shape[1] + g_ref.shape[1]
    row_groups = (x_ref.shape[0] - keep) // GROUP_ROWS
    share_cols = out_ref.shape[2]
    for share, row, start in shares(row_groups, joint // share_cols, share_cols):
        rows = pl.ds(keep + row, GROUP_ROWS)
        split = min(max(width - start, 0), share_cols)
        if split > 0:
            out_ref[share, :, pl.ds(0, split)] = x_ref[rows, pl.ds(start, split)]
        if split < share_cols:
            out_ref[share, :, pl.ds(split, share_cols - split)] = g_ref[
                rows, pl.ds(start + split - width, share_cols - split)
            ]


def term_kernel(keep, lengths_ref, x_ref, g_ref, seg_col_ref, seg_row_ref, term_ref, y_ref):
    width = g_ref.shape[1]
    rows_all = x_ref.shape[0]

    def rows_of(rows, allowed, counts):
        values, queries, key_rows = (x_ref[rows, pl.ds((1 + i) * width, width)] for i in range(3))
        normed = forward(values, queries, key_rows, allowed, counts)[3]
        y_ref[rows, :] = (normed * x_ref[rows, pl.ds(0, width)].astype(F32)).astype(BF16)

    moved = rows_all - keep
    total, ends = 0, []
    for i in range(lengths_ref.shape[1]):
        total = total + lengths_ref[0, i]
        ends.append(total)
    rows_of(pl.ds(keep, moved), *masks(segments_of(ends, (moved, 1), 0), segments_of(ends, (1, moved), 1)))
    rows_of(pl.ds(0, keep), *masks(seg_col_ref[...], seg_row_ref[...]))
    blocks, _, block_cols = term_ref.shape
    joined = max(1, 256 // block_cols)
    for b in range(0, blocks, joined):
        found = dot(g_ref[...], y_ref[:, pl.ds(b * block_cols, joined * block_cols)], ((0,), (0,)))
        for i in range(joined):
            term_ref[b + i] = found[:, i * block_cols : (i + 1) * block_cols].astype(BF16)


def back_kernel(keep, lengths_ref, x_ref, g_ref, came_ref, w_ref, seg_col_ref, seg_row_ref, out_ref, block_ref):
    width = g_ref.shape[1]
    moved, joint = block_ref.shape
    share_cols = came_ref.shape[2]
    for share, row, start in shares(moved // GROUP_ROWS, joint // share_cols, share_cols):
        block_ref[pl.ds(row, GROUP_ROWS), pl.ds(start, share_cols)] = came_ref[share]

    def put_in(rows):
        def put(part, cols, found):
            out_ref[rows, pl.ds(part * width + cols.start, cols.stop - cols.start)] = found.astype(BF16)

        return put

    total, ends = 0, []
    for i in range(lengths_ref.shape[1]):
        total = total + lengths_ref[0, i]
        ends.append(total)
    kept_grad_y = dot(g_ref[pl.ds(0, keep), :], w_ref[...], ((1,), (0,)))
    parts = [x_ref[pl.ds(0, keep), pl.ds(i * width, width)] for i in range(4)]
    backward(*parts, kept_grad_y, *masks(seg_col_ref[...], seg_row_ref[...]), put_in(pl.ds(0, keep)))
    *parts, grads = [block_ref[:, pl.ds(i * width, width)] for i in range(5)]
    grad_y = dot(grads, w_ref[...], ((1,), (0,)))
    backward(
        *parts,
        grad_y,
        *masks(segments_of(ends, (moved, 1), 0), segments_of(ends, (1, moved), 1)),
        put_in(pl.ds(keep, moved)),
    )


VMEM = pl.BlockSpec(memory_space=pltpu.VMEM)
SMEM = pl.BlockSpec(memory_space=pltpu.SMEM)
PARAMS = pltpu.CompilerParams(vmem_limit_bytes=40 * 2**20)


def cost(flops, nbytes):
    return pl.CostEstimate(flops=flops, bytes_accessed=nbytes, transcendentals=0)


def permuted(value, axis, target):
    size = lax.axis_size(axis)
    return lax.ppermute(value, axis, [(i, target(i)) for i in range(size)])


def pick(value, index, dim=0):
    return lax.dynamic_index_in_dim(value, index, dim, keepdims=False)


def added(*values):
    return functools.reduce(jnp.add, [value.astype(F32) for value in values])


def scatter_sum(value, axis):
    size, me = lax.axis_size(axis), lax.axis_index(axis)
    came = [
        permuted(pick(value, (me + step) & (size - 1)), axis, lambda i, step=step: (i + step) % size)
        for step in range(1, size)
    ]
    return added(pick(value, me), *came).astype(BF16)


def ring_of_rings_sum(value, axis, inner):
    size, me = lax.axis_size(axis), lax.axis_index(axis)
    outer = size // inner
    value = value.reshape((outer, inner) + value.shape[1:])
    low, high = me & (inner - 1), me >> (inner.bit_length() - 1)
    came = [
        permuted(
            pick(value, (low + step) & (inner - 1), 1),
            axis,
            lambda i, step=step: i // inner * inner + (i + step) % inner,
        )
        for step in range(1, inner)
    ]
    value = added(pick(value, low, 1), *came).astype(BF16)
    came = [
        permuted(pick(value, (high + step) & (outer - 1)), axis, lambda i, step=step: (i + step * inner) % size)
        for step in range(1, outer)
    ]
    return added(pick(value, high), *came)


def exchange(value, axes=DP):
    return lax.all_to_all(value, axes, split_axis=0, concat_axis=0, tiled=True)


def local(uvqk, grad_out, w_out, kept_segments, moved_lengths, dest_device):
    keep = kept_segments.shape[1]
    rows, width = grad_out.shape
    moved = rows - keep
    n_x, n_y, n_core, n_z = (lax.axis_size(a) for a in ("x", "y", "core", "z"))
    groups = n_x * n_y * n_core
    dp_index, z_index = lax.axis_index(DP), lax.axis_index("z")
    indices = jnp.arange(groups, dtype=jnp.int32)
    source_of = jnp.sum(jnp.where(dest_device[None, :] == indices[:, None], indices[None, :], 0), axis=1)
    own_source = jnp.sum(jnp.where(dest_device == dp_index, indices, 0))
    own_lengths = lax.dynamic_slice_in_dim(moved_lengths, dp_index * n_z + z_index, 1, 0)
    recv_lengths = lax.dynamic_slice_in_dim(moved_lengths, own_source * n_z + z_index, 1, 0)
    seg_col, seg_row = kept_segments.reshape(keep, 1), kept_segments

    w_all = lax.all_gather(w_out, "z", axis=0, tiled=True)
    share_cols = 5 * width * (moved // GROUP_ROWS) // groups
    block = pl.pallas_call(
        functools.partial(pack_kernel, keep),
        out_shape=jax.ShapeDtypeStruct((groups, GROUP_ROWS, share_cols), BF16),
        in_specs=[VMEM, VMEM],
        out_specs=VMEM,
        compiler_params=PARAMS,
        cost_estimate=cost(0, 8 * width),
        name="pack",
    )(uvqk, grad_out)
    uvqk, grad_out, block = lax.optimization_barrier((uvqk, grad_out, block))
    block = exchange(block)

    blocks = n_core * n_x
    block_cols = width // blocks
    term = pl.pallas_call(
        functools.partial(term_kernel, keep),
        out_shape=jax.ShapeDtypeStruct((blocks, width, block_cols), BF16),
        in_specs=[SMEM, VMEM, VMEM, VMEM, VMEM],
        out_specs=VMEM,
        scratch_shapes=[pltpu.VMEM((rows, width), BF16)],
        compiler_params=PARAMS,
        cost_estimate=cost(0, 8 * width),
        name="term",
    )(own_lengths, uvqk, grad_out, seg_col, seg_row)
    part = scatter_sum(term.reshape(n_core, n_x, width, block_cols), "core")
    part = scatter_sum(part, "x")
    own_rows = width // n_z
    part, block = lax.optimization_barrier((part, block))
    block = exchange(block[source_of])
    part = ring_of_rings_sum(part.reshape(n_z, own_rows, block_cols), "z", min(4, n_z))
    part = lax.optimization_barrier((part, block))[0]
    part = exchange(part.reshape(n_y, own_rows // n_y, block_cols), "y")
    part = (jnp.sum(part, axis=0) * (1.0 / (groups * n_z))).astype(BF16)
    spread = exchange(jnp.broadcast_to(part[None], (groups,) + part.shape))
    spread = spread.astype(F32).reshape(n_x, n_y, n_core, own_rows // n_y, block_cols)
    grad_weight = spread.transpose(1, 3, 2, 0, 4).reshape(own_rows, width)

    grad_rows = pl.pallas_call(
        functools.partial(back_kernel, keep),
        out_shape=jax.ShapeDtypeStruct(uvqk.shape, BF16),
        in_specs=[SMEM] + [VMEM] * 6,
        out_specs=VMEM,
        scratch_shapes=[pltpu.VMEM((moved, 5 * width), BF16)],
        compiler_params=PARAMS,
        cost_estimate=cost(8 * rows * width * width, 8 * width * width),
        name="back",
    )(recv_lengths, uvqk, grad_out, block, w_all, seg_col, seg_row)
    return grad_rows, grad_weight


def fine_mesh(mesh):
    n_dp, n_z = mesh.devices.shape
    n_core = 2
    n_x = min(4, n_dp // 4)
    shape = (n_x, n_dp // (n_x * n_core), n_core, n_z)
    return Mesh(mesh.devices.reshape(shape), ("x", "y", "core", "z"))


def solution(mesh):
    everyone = P(("x", "y", "core", "z"), None)
    placed = (everyone, everyone, P("z", None), everyone, P(), P())
    return jax.shard_map(
        local,
        mesh=fine_mesh(mesh),
        in_specs=placed,
        out_specs=(everyone, P("z", None)),
        check_vma=False,
    )
```

```python
import functools
import math

import jax
import jax.numpy as jnp
from jax import lax
from jax.experimental import pallas as pl
from jax.experimental.pallas import tpu as pltpu
from jax.sharding import Mesh
from jax.sharding import PartitionSpec as P

HEADS = 4
EPS = 1e-05
GROUP_ROWS = 16
BF16 = jnp.bfloat16
F32 = jnp.float32
DP = ("x", "y", "core")


def dot(a, b, dims):
    return lax.dot_general(a, b, (dims, ((), ())), preferred_element_type=F32)


def segments_of(ends, shape, dim):
    places = lax.broadcasted_iota(jnp.int32, shape, dim)
    passed = jnp.zeros(shape, jnp.int32)
    for end in ends:
        passed = passed + (places >= end).astype(jnp.int32)
    return jnp.where(passed == len(ends), -1, passed)


def masks(seg_column, seg_row):
    length = seg_column.shape[0]
    square = (length, length)
    same = seg_column == seg_row
    earlier = lax.broadcasted_iota(jnp.int32, square, 1) <= lax.broadcasted_iota(jnp.int32, square, 0)
    allowed = same & earlier & (seg_column >= 0)
    counts = jnp.sum(same.astype(F32), axis=1, keepdims=True)
    return allowed, counts


def forward(values, queries, key_rows, allowed, counts):
    width = values.shape[1]
    head_dim = width // HEADS
    scale = 1.0 / math.sqrt(head_dim)
    scores, sigmas, weights, mixed = [], [], [], []
    for h in range(HEADS):
        cols = slice(h * head_dim, (h + 1) * head_dim)
        s = dot(queries[:, cols], key_rows[:, cols], ((1,), (1,))) * scale
        sigma = jax.nn.sigmoid(s)
        w = (jnp.where(allowed, s * sigma, 0.0) / counts).astype(BF16)
        scores.append(s)
        sigmas.append(sigma)
        weights.append(w)
        mixed.append(dot(w, values[:, cols], ((1,), (0,))))
    mixed = jnp.concatenate(mixed, axis=1)
    centered = mixed - jnp.mean(mixed, axis=1, keepdims=True)
    inverse = lax.rsqrt(jnp.mean(centered * centered, axis=1, keepdims=True) + EPS)
    return scores, sigmas, weights, centered * inverse, inverse


def backward(gate, values, queries, key_rows, grad_y, allowed, counts, put):
    width = values.shape[1]
    head_dim = width // HEADS
    scale = 1.0 / math.sqrt(head_dim)
    scores, sigmas, weights, normed, inverse = forward(values, queries, key_rows, allowed, counts)
    put(0, slice(0, width), grad_y * normed)
    grad_normed = grad_y * gate.astype(F32)
    grad_mixed = inverse * (
        grad_normed
        - jnp.mean(grad_normed, axis=1, keepdims=True)
        - normed * jnp.mean(grad_normed * normed, axis=1, keepdims=True)
    )
    grad_mixed = grad_mixed.astype(BF16)
    factor = scale / counts
    for h in range(HEADS):
        cols = slice(h * head_dim, (h + 1) * head_dim)
        s, sigma = scores[h], sigmas[h]
        grad_weights = dot(grad_mixed[:, cols], values[:, cols], ((1,), (1,)))
        put(1, cols, dot(weights[h], grad_mixed[:, cols], ((0,), (0,))))
        slope = sigma * (1.0 + s * (1.0 - sigma))
        grad_scores = (jnp.where(allowed, grad_weights * slope, 0.0) * factor).astype(BF16)
        put(2, cols, dot(grad_scores, key_rows[:, cols], ((1,), (0,))))
        put(3, cols, dot(grad_scores, queries[:, cols], ((0,), (0,))))


def shares(row_groups, col_groups, share_cols):
    for r in range(row_groups):
        for c in range(col_groups):
            yield r * col_groups + c, r * GROUP_ROWS, c * share_cols


def pack_kernel(keep, x_ref, g_ref, out_ref, block_ref, sems):
    width, joint = x_ref.shape[1], block_ref.shape[1]
    moved = block_ref.shape[0]
    share_cols = out_ref.shape[2]
    rows = pl.ds(keep, moved)
    from_x = pltpu.make_async_copy(x_ref.at[rows], block_ref.at[:, pl.ds(0, width)], sems.at[0])
    from_g = pltpu.make_async_copy(g_ref.at[rows], block_ref.at[:, pl.ds(width, joint - width)], sems.at[1])
    from_x.start()
    from_g.start()
    from_x.wait()
    from_g.wait()
    for share, row, start in shares(moved // GROUP_ROWS, joint // share_cols, share_cols):
        out_ref[share] = block_ref[pl.ds(row, GROUP_ROWS), pl.ds(start, share_cols)]


def term_kernel(keep, core_ref, lengths_ref, x_ref, g_ref, seg_col_ref, seg_row_ref, mine_ref, other_ref, y_ref):
    width = g_ref.shape[1]
    rows_all = x_ref.shape[0]

    def rows_of(rows, allowed, counts):
        values, queries, key_rows = (x_ref[rows, pl.ds((1 + i) * width, width)] for i in range(3))
        normed = forward(values, queries, key_rows, allowed, counts)[3]
        y_ref[rows, :] = (normed * x_ref[rows, pl.ds(0, width)].astype(F32)).astype(BF16)

    moved = rows_all - keep
    total, ends = 0, []
    for i in range(lengths_ref.shape[1]):
        total = total + lengths_ref[0, i]
        ends.append(total)
    rows_of(pl.ds(keep, moved), *masks(segments_of(ends, (moved, 1), 0), segments_of(ends, (1, moved), 1)))
    rows_of(pl.ds(0, keep), *masks(seg_col_ref[...], seg_row_ref[...]))
    blocks, _, block_cols = mine_ref.shape
    joined = max(1, 256 // block_cols)
    core = core_ref[0]
    for half, term_ref in ((core, mine_ref), (1 - core, other_ref)):
        for b in range(0, blocks, joined):
            start = pl.multiple_of((half * blocks + b) * block_cols, 128)
            found = dot(g_ref[...], y_ref[:, pl.ds(start, joined * block_cols)], ((0,), (0,)))
            for i in range(joined):
                term_ref[b + i] = found[:, i * block_cols : (i + 1) * block_cols].astype(BF16)


def back_kernel(keep, lengths_ref, x_ref, g_ref, came_ref, w_ref, seg_col_ref, seg_row_ref, out_ref, block_ref):
    width = g_ref.shape[1]
    moved, joint = block_ref.shape
    share_cols = came_ref.shape[2]
    for share, row, start in shares(moved // GROUP_ROWS, joint // share_cols, share_cols):
        block_ref[pl.ds(row, GROUP_ROWS), pl.ds(start, share_cols)] = came_ref[share]

    def put_in(rows):
        def put(part, cols, found):
            out_ref[rows, pl.ds(part * width + cols.start, cols.stop - cols.start)] = found.astype(BF16)

        return put

    total, ends = 0, []
    for i in range(lengths_ref.shape[1]):
        total = total + lengths_ref[0, i]
        ends.append(total)
    kept_grad_y = dot(g_ref[pl.ds(0, keep), :], w_ref[...], ((1,), (0,)))
    parts = [x_ref[pl.ds(0, keep), pl.ds(i * width, width)] for i in range(4)]
    backward(*parts, kept_grad_y, *masks(seg_col_ref[...], seg_row_ref[...]), put_in(pl.ds(0, keep)))
    *parts, grads = [block_ref[:, pl.ds(i * width, width)] for i in range(5)]
    grad_y = dot(grads, w_ref[...], ((1,), (0,)))
    backward(
        *parts,
        grad_y,
        *masks(segments_of(ends, (moved, 1), 0), segments_of(ends, (1, moved), 1)),
        put_in(pl.ds(keep, moved)),
    )


VMEM = pl.BlockSpec(memory_space=pltpu.VMEM)
HBM = pl.BlockSpec(memory_space=pltpu.HBM)
SMEM = pl.BlockSpec(memory_space=pltpu.SMEM)
PARAMS = pltpu.CompilerParams(vmem_limit_bytes=24 * 2**20)


def cost(flops, nbytes):
    return pl.CostEstimate(flops=flops, bytes_accessed=nbytes, transcendentals=0)


def permuted(value, axis, target):
    size = lax.axis_size(axis)
    return lax.ppermute(value, axis, [(i, target(i)) for i in range(size)])


def pick(value, index, dim=0):
    return lax.dynamic_index_in_dim(value, index, dim, keepdims=False)


def added(*values):
    return functools.reduce(jnp.add, [value.astype(F32) for value in values])


def scatter_sum(value, axis):
    size, me = lax.axis_size(axis), lax.axis_index(axis)
    came = [
        permuted(pick(value, (me + step) & (size - 1)), axis, lambda i, step=step: (i + step) % size)
        for step in range(1, size)
    ]
    return added(pick(value, me), *came).astype(BF16)


def ring_of_four_sum(value, axis):
    size, me = lax.axis_size(axis), lax.axis_index(axis)
    if size != 4:
        done = scatter_sum(value, axis)
        return done, [done]
    half = value.shape[1] // 2
    halves = []
    for rows, first, second in ((value[:, :half], 1, 3), (value[:, half:], 3, 1)):
        sent = jnp.stack([pick(rows, me ^ first), pick(rows, me ^ 2)])
        held = jnp.stack([pick(rows, me), pick(rows, me ^ second)])
        halves.append((permuted(sent, axis, lambda i, first=first: i ^ first), held, second))
    first_round = [added(held, came).astype(BF16) for came, held, _ in halves]
    done = []
    for held, (_, _, second) in zip(first_round, halves):
        came = permuted(held[1], axis, lambda i, second=second: i ^ second)
        done.append(added(held[0], came).astype(BF16))
    return jnp.concatenate(done), first_round


def ring_of_rings_sum(value, axis, inner):
    size, me = lax.axis_size(axis), lax.axis_index(axis)
    outer = size // inner
    value = value.reshape((outer, inner) + value.shape[1:])
    low, high = me & (inner - 1), me >> (inner.bit_length() - 1)
    came = [
        permuted(
            pick(value, (low + step) & (inner - 1), 1),
            axis,
            lambda i, step=step: i // inner * inner + (i + step) % inner,
        )
        for step in range(1, inner)
    ]
    value = added(pick(value, low, 1), *came).astype(BF16)
    came = [
        permuted(pick(value, (high + step) & (outer - 1)), axis, lambda i, step=step: (i + step * inner) % size)
        for step in range(1, outer)
    ]
    return added(pick(value, high), *came)


def exchange(value, axes=DP):
    return lax.all_to_all(value, axes, split_axis=0, concat_axis=0, tiled=True)


def local(uvqk, grad_out, w_out, kept_segments, moved_lengths, dest_device):
    keep = kept_segments.shape[1]
    rows, width = grad_out.shape
    moved = rows - keep
    n_x, n_y, n_core, n_z = (lax.axis_size(a) for a in ("x", "y", "core", "z"))
    groups = n_x * n_y * n_core
    dp_index, z_index = lax.axis_index(DP), lax.axis_index("z")
    indices = jnp.arange(groups, dtype=jnp.int32)
    source_of = jnp.sum(jnp.where(dest_device[None, :] == indices[:, None], indices[None, :], 0), axis=1)
    own_source = jnp.sum(jnp.where(dest_device == dp_index, indices, 0))
    own_lengths = lax.dynamic_slice_in_dim(moved_lengths, dp_index * n_z + z_index, 1, 0)
    recv_lengths = lax.dynamic_slice_in_dim(moved_lengths, own_source * n_z + z_index, 1, 0)
    seg_col, seg_row = kept_segments.reshape(keep, 1), kept_segments

    w_all = lax.all_gather(w_out, "z", axis=0, tiled=True)
    share_cols = 5 * width * (moved // GROUP_ROWS) // groups
    block = pl.pallas_call(
        functools.partial(pack_kernel, keep),
        out_shape=jax.ShapeDtypeStruct((groups, GROUP_ROWS, share_cols), BF16),
        in_specs=[HBM, HBM],
        out_specs=VMEM,
        scratch_shapes=[pltpu.VMEM((moved, 5 * width), BF16), pltpu.SemaphoreType.DMA((2,))],
        compiler_params=pltpu.CompilerParams(vmem_limit_bytes=60 * 2**20),
        cost_estimate=cost(0, 8 * width),
        name="pack",
    )(uvqk, grad_out)
    uvqk, grad_out, block = lax.optimization_barrier((uvqk, grad_out, block))
    block = exchange(block)

    block_cols = width // (n_core * n_x)
    core_half = jax.ShapeDtypeStruct((n_x, width, block_cols), BF16)
    mine, other = pl.pallas_call(
        functools.partial(term_kernel, keep),
        out_shape=(core_half, core_half),
        in_specs=[SMEM, SMEM, VMEM, VMEM, VMEM, VMEM],
        out_specs=(VMEM, VMEM),
        scratch_shapes=[pltpu.VMEM((rows, width), BF16)],
        compiler_params=PARAMS,
        cost_estimate=cost(0, 8 * width),
        name="term",
    )(lax.axis_index("core").reshape(1), own_lengths, uvqk, grad_out, seg_col, seg_row)
    part = added(mine, permuted(other, "core", lambda i: i ^ 1)).astype(BF16)
    part, first_round = ring_of_four_sum(part, "x")
    own_rows = width // n_z
    block = lax.optimization_barrier((block, first_round))[0]
    block = block[source_of]
    part, block = lax.optimization_barrier((part, block))
    block = exchange(block)
    part = ring_of_rings_sum(part.reshape(n_z, own_rows, block_cols), "z", min(4, n_z))
    part = lax.optimization_barrier((part, block))[0]
    part = exchange(part.reshape(n_y, own_rows // n_y, block_cols), "y")
    part = (jnp.sum(part, axis=0) * (1.0 / (groups * n_z))).astype(BF16)
    spread = exchange(jnp.broadcast_to(part[None], (groups,) + part.shape))
    spread = spread.astype(F32).reshape(n_x, n_y, n_core, own_rows // n_y, block_cols)
    grad_weight = spread.transpose(1, 3, 2, 0, 4).reshape(own_rows, width)

    grad_rows = pl.pallas_call(
        functools.partial(back_kernel, keep),
        out_shape=jax.ShapeDtypeStruct(uvqk.shape, BF16),
        in_specs=[SMEM] + [VMEM] * 6,
        out_specs=VMEM,
        scratch_shapes=[pltpu.VMEM((moved, 5 * width), BF16)],
        compiler_params=PARAMS,
        cost_estimate=cost(8 * rows * width * width, 8 * width * width),
        name="back",
    )(recv_lengths, uvqk, grad_out, block, w_all, seg_col, seg_row)
    return grad_rows, grad_weight


def fine_mesh(mesh):
    n_dp, n_z = mesh.devices.shape
    n_core = 2
    n_x = min(4, n_dp // 4)
    shape = (n_x, n_dp // (n_x * n_core), n_core, n_z)
    return Mesh(mesh.devices.reshape(shape), ("x", "y", "core", "z"))


def solution(mesh):
    everyone = P(("x", "y", "core", "z"), None)
    placed = (everyone, everyone, P("z", None), everyone, P(), P())
    return jax.shard_map(
        local,
        mesh=fine_mesh(mesh),
        in_specs=placed,
        out_specs=(everyone, P("z", None)),
        check_vma=False,
    )
```

```python
import functools
import math

import jax
import jax.numpy as jnp
from jax import lax
from jax.experimental import pallas as pl
from jax.experimental.pallas import tpu as pltpu
from jax.sharding import Mesh
from jax.sharding import PartitionSpec as P

HEADS = 4
EPS = 1e-05
GROUP_ROWS = 16
BF16 = jnp.bfloat16
F32 = jnp.float32
DP = ("x", "y", "core")


def dot(a, b, dims):
    return lax.dot_general(a, b, (dims, ((), ())), preferred_element_type=F32)


def segments_of(ends, shape, dim):
    places = lax.broadcasted_iota(jnp.int32, shape, dim)
    passed = jnp.zeros(shape, jnp.int32)
    for end in ends:
        passed = passed + (places >= end).astype(jnp.int32)
    return jnp.where(passed == len(ends), -1, passed)


def masks(seg_column, seg_row):
    length = seg_column.shape[0]
    square = (length, length)
    same = seg_column == seg_row
    earlier = lax.broadcasted_iota(jnp.int32, square, 1) <= lax.broadcasted_iota(jnp.int32, square, 0)
    allowed = same & earlier & (seg_column >= 0)
    counts = jnp.sum(same.astype(F32), axis=1, keepdims=True)
    return allowed, counts


def forward(values, queries, key_rows, allowed, counts):
    width = values.shape[1]
    head_dim = width // HEADS
    scale = 1.0 / math.sqrt(head_dim)
    scores, sigmas, weights, mixed = [], [], [], []
    for h in range(HEADS):
        cols = slice(h * head_dim, (h + 1) * head_dim)
        s = dot(queries[:, cols], key_rows[:, cols], ((1,), (1,))) * scale
        sigma = jax.nn.sigmoid(s)
        w = (jnp.where(allowed, s * sigma, 0.0) / counts).astype(BF16)
        scores.append(s)
        sigmas.append(sigma)
        weights.append(w)
        mixed.append(dot(w, values[:, cols], ((1,), (0,))))
    mixed = jnp.concatenate(mixed, axis=1)
    centered = mixed - jnp.mean(mixed, axis=1, keepdims=True)
    inverse = lax.rsqrt(jnp.mean(centered * centered, axis=1, keepdims=True) + EPS)
    return scores, sigmas, weights, centered * inverse, inverse


def backward(gate, values, queries, key_rows, grad_y, allowed, counts, put):
    width = values.shape[1]
    head_dim = width // HEADS
    scale = 1.0 / math.sqrt(head_dim)
    scores, sigmas, weights, normed, inverse = forward(values, queries, key_rows, allowed, counts)
    put(0, slice(0, width), grad_y * normed)
    grad_normed = grad_y * gate.astype(F32)
    grad_mixed = inverse * (
        grad_normed
        - jnp.mean(grad_normed, axis=1, keepdims=True)
        - normed * jnp.mean(grad_normed * normed, axis=1, keepdims=True)
    )
    grad_mixed = grad_mixed.astype(BF16)
    factor = scale / counts
    for h in range(HEADS):
        cols = slice(h * head_dim, (h + 1) * head_dim)
        s, sigma = scores[h], sigmas[h]
        grad_weights = dot(grad_mixed[:, cols], values[:, cols], ((1,), (1,)))
        put(1, cols, dot(weights[h], grad_mixed[:, cols], ((0,), (0,))))
        slope = sigma * (1.0 + s * (1.0 - sigma))
        grad_scores = (jnp.where(allowed, grad_weights * slope, 0.0) * factor).astype(BF16)
        put(2, cols, dot(grad_scores, key_rows[:, cols], ((1,), (0,))))
        put(3, cols, dot(grad_scores, queries[:, cols], ((0,), (0,))))


def shares(row_groups, col_groups, share_cols):
    for r in range(row_groups):
        for c in range(col_groups):
            yield r * col_groups + c, r * GROUP_ROWS, c * share_cols


def pack_kernel(keep, x_ref, g_ref, out_ref, block_ref, sems):
    width, joint = x_ref.shape[1], block_ref.shape[1]
    moved = block_ref.shape[0]
    share_cols = out_ref.shape[2]
    rows = pl.ds(keep, moved)
    from_x = pltpu.make_async_copy(x_ref.at[rows], block_ref.at[:, pl.ds(0, width)], sems.at[0])
    from_g = pltpu.make_async_copy(g_ref.at[rows], block_ref.at[:, pl.ds(width, joint - width)], sems.at[1])
    from_x.start()
    from_g.start()
    from_x.wait()
    from_g.wait()
    for share, row, start in shares(moved // GROUP_ROWS, joint // share_cols, share_cols):
        out_ref[share] = block_ref[pl.ds(row, GROUP_ROWS), pl.ds(start, share_cols)]


def term_kernel(keep, lengths_ref, x_ref, g_ref, seg_col_ref, seg_row_ref, term_ref, y_ref):
    width = g_ref.shape[1]
    rows_all = x_ref.shape[0]

    def rows_of(rows, allowed, counts):
        values, queries, key_rows = (x_ref[rows, pl.ds((1 + i) * width, width)] for i in range(3))
        normed = forward(values, queries, key_rows, allowed, counts)[3]
        y_ref[rows, :] = (normed * x_ref[rows, pl.ds(0, width)].astype(F32)).astype(BF16)

    moved = rows_all - keep
    total, ends = 0, []
    for i in range(lengths_ref.shape[1]):
        total = total + lengths_ref[0, i]
        ends.append(total)
    rows_of(pl.ds(keep, moved), *masks(segments_of(ends, (moved, 1), 0), segments_of(ends, (1, moved), 1)))
    rows_of(pl.ds(0, keep), *masks(seg_col_ref[...], seg_row_ref[...]))
    for start in range(0, width, 256):
        cols = pl.ds(start, 256)
        term_ref[:, cols] = dot(g_ref[...], y_ref[:, cols], ((0,), (0,))).astype(BF16)


def back_kernel(
    keep, where_ref, lengths_ref, x_ref, g_ref, came_ref, w_mine_ref, w_other_ref, seg_col_ref, seg_row_ref,
    out_ref, block_ref, grads_ref, grad_y_ref
):
    width = g_ref.shape[1]
    moved, joint = block_ref.shape
    share_cols = came_ref.shape[2]
    for share, row, start in shares(moved // GROUP_ROWS, joint // share_cols, share_cols):
        block_ref[pl.ds(row, GROUP_ROWS), pl.ds(start, share_cols)] = came_ref[share]
    grads_ref[pl.ds(0, keep), :] = g_ref[pl.ds(0, keep), :]
    grads_ref[pl.ds(keep, moved), :] = block_ref[:, pl.ds(joint - width, width)]
    core, x = where_ref[0], where_ref[1]
    blocks, _, block_cols = w_mine_ref.shape
    for half, w_ref in ((core, w_mine_ref), (1 - core, w_other_ref)):
        for step in range(blocks):
            start = pl.multiple_of((half * blocks + (x ^ step)) * block_cols, 128)
            grad_y_ref[:, pl.ds(start, block_cols)] = dot(grads_ref[...], w_ref[step], ((1,), (0,)))

    def put_in(rows):
        def put(part, cols, found):
            out_ref[rows, pl.ds(part * width + cols.start, cols.stop - cols.start)] = found.astype(BF16)

        return put

    total, ends = 0, []
    for i in range(lengths_ref.shape[1]):
        total = total + lengths_ref[0, i]
        ends.append(total)
    parts = [x_ref[pl.ds(0, keep), pl.ds(i * width, width)] for i in range(4)]
    backward(*parts, grad_y_ref[pl.ds(0, keep), :], *masks(seg_col_ref[...], seg_row_ref[...]), put_in(pl.ds(0, keep)))
    parts = [block_ref[:, pl.ds(i * width, width)] for i in range(4)]
    backward(
        *parts,
        grad_y_ref[pl.ds(keep, moved), :],
        *masks(segments_of(ends, (moved, 1), 0), segments_of(ends, (1, moved), 1)),
        put_in(pl.ds(keep, moved)),
    )


VMEM = pl.BlockSpec(memory_space=pltpu.VMEM)
HBM = pl.BlockSpec(memory_space=pltpu.HBM)
SMEM = pl.BlockSpec(memory_space=pltpu.SMEM)
PARAMS = pltpu.CompilerParams(vmem_limit_bytes=24 * 2**20)


def cost(flops, nbytes):
    return pl.CostEstimate(flops=flops, bytes_accessed=nbytes, transcendentals=0)


def permuted(value, axis, target):
    size = lax.axis_size(axis)
    return lax.ppermute(value, axis, [(i, target(i)) for i in range(size)])


def pick(value, index, dim=0):
    return lax.dynamic_index_in_dim(value, index, dim, keepdims=False)


def added(*values):
    return functools.reduce(jnp.add, [value.astype(F32) for value in values])


def doubling_gather(value, axis):
    me = lax.axis_index(axis)
    value = value[None]
    for step in range(lax.axis_size(axis).bit_length() - 1):
        came = permuted(value, axis, lambda i, step=step: i ^ (1 << step))
        low = ((me >> step) & 1) == 0
        value = jnp.concatenate([jnp.where(low, value, came), jnp.where(low, came, value)])
    return value


def exchange(value, axes=DP):
    return lax.all_to_all(value, axes, split_axis=0, concat_axis=0, tiled=True)


def local(uvqk, grad_out, w_out, kept_segments, moved_lengths, dest_device):
    keep = kept_segments.shape[1]
    rows, width = grad_out.shape
    moved = rows - keep
    n_x, n_y, n_core, n_z = (lax.axis_size(a) for a in ("x", "y", "core", "z"))
    groups = n_x * n_y * n_core
    dp_index, z_index = lax.axis_index(DP), lax.axis_index("z")
    indices = jnp.arange(groups, dtype=jnp.int32)
    seg_col, seg_row = kept_segments.reshape(keep, 1), kept_segments

    share_cols = 5 * width * (moved // GROUP_ROWS) // groups
    block = pl.pallas_call(
        functools.partial(pack_kernel, keep),
        out_shape=jax.ShapeDtypeStruct((groups, GROUP_ROWS, share_cols), BF16),
        in_specs=[HBM, HBM],
        out_specs=VMEM,
        scratch_shapes=[pltpu.VMEM((moved, 5 * width), BF16), pltpu.SemaphoreType.DMA((2,))],
        compiler_params=pltpu.CompilerParams(vmem_limit_bytes=60 * 2**20),
        cost_estimate=cost(0, 8 * width),
        name="pack",
    )(uvqk, grad_out)
    uvqk, grad_out, dest_device, block = lax.optimization_barrier((uvqk, grad_out, dest_device, block))
    block = exchange(block)

    source_of = jnp.sum(jnp.where(dest_device[None, :] == indices[:, None], indices[None, :], 0), axis=1)
    own_source = jnp.sum(jnp.where(dest_device == dp_index, indices, 0))
    own_lengths = lax.dynamic_slice_in_dim(moved_lengths, dp_index * n_z + z_index, 1, 0)
    recv_lengths = lax.dynamic_slice_in_dim(moved_lengths, own_source * n_z + z_index, 1, 0)
    term = pl.pallas_call(
        functools.partial(term_kernel, keep),
        out_shape=jax.ShapeDtypeStruct((width, width), BF16),
        in_specs=[SMEM, VMEM, VMEM, VMEM, VMEM],
        out_specs=VMEM,
        scratch_shapes=[pltpu.VMEM((rows, width), BF16)],
        compiler_params=PARAMS,
        cost_estimate=cost(0, 8 * width),
        name="term",
    )(own_lengths, uvqk, grad_out, seg_col, seg_row)
    x, core = lax.axis_index("x"), lax.axis_index("core")
    block_cols = width // (n_core * n_x)
    w_mine = lax.dynamic_slice_in_dim(w_out, (core * n_x + x) * block_cols, block_cols, 1)
    w_mine, term = lax.optimization_barrier((w_mine, term))
    w_mine = doubling_gather(w_mine, "z").reshape(width, block_cols)
    part = lax.psum_scatter(term, "z", scatter_dimension=0, tiled=True)

    block, w_mine = lax.optimization_barrier((block[source_of], w_mine))
    block = exchange(block)
    others = [permuted(w_mine, "x", lambda i, step=step: i ^ step) for step in range(1, n_x)]
    w_mine = jnp.stack([w_mine, *others])
    w_other = permuted(w_mine, "core", lambda i: i ^ 1)

    tile_rows = width // n_z // 8
    slot_cols = width * 8 // groups
    part = lax.optimization_barrier((part, block))[0]
    part = part.reshape(8, tile_rows, width // slot_cols, slot_cols).transpose(0, 2, 1, 3)
    part = exchange(part.reshape(groups, tile_rows, slot_cols))
    part = (jnp.sum(part.astype(F32), axis=0) * (1.0 / (groups * n_z))).astype(BF16)
    spread = exchange(jnp.broadcast_to(part[None], (groups,) + part.shape)).astype(F32)
    spread = spread.reshape(8, groups // 8, tile_rows, slot_cols).transpose(0, 2, 1, 3)
    grad_weight = spread.reshape(width // n_z, width)

    grad_rows = pl.pallas_call(
        functools.partial(back_kernel, keep),
        out_shape=jax.ShapeDtypeStruct(uvqk.shape, BF16),
        in_specs=[SMEM, SMEM] + [VMEM] * 7,
        out_specs=VMEM,
        scratch_shapes=[
            pltpu.VMEM((moved, 5 * width), BF16),
            pltpu.VMEM((rows, width), BF16),
            pltpu.VMEM((rows, width), F32),
        ],
        compiler_params=PARAMS,
        cost_estimate=cost(8 * rows * width * width, 8 * width * width),
        name="back",
    )(jnp.stack([core, x]), recv_lengths, uvqk, grad_out, block, w_mine, w_other, seg_col, seg_row)
    return grad_rows, grad_weight


def fine_mesh(mesh):
    n_dp, n_z = mesh.devices.shape
    n_core = 2
    n_x = min(4, n_dp // 4)
    shape = (n_x, n_dp // (n_x * n_core), n_core, n_z)
    return Mesh(mesh.devices.reshape(shape), ("x", "y", "core", "z"))


def solution(mesh):
    everyone = P(("x", "y", "core", "z"), None)
    placed = (everyone, everyone, P("z", None), everyone, P(), P())
    return jax.shard_map(
        local,
        mesh=fine_mesh(mesh),
        in_specs=placed,
        out_specs=(everyone, P("z", None)),
        check_vma=False,
    )
```

```python
import functools
import math

import jax
import jax.numpy as jnp
from jax import lax
from jax.experimental import pallas as pl
from jax.experimental.pallas import tpu as pltpu
from jax.sharding import Mesh
from jax.sharding import PartitionSpec as P

HEADS = 4
EPS = 1e-05
GROUP_ROWS = 16
BF16 = jnp.bfloat16
F32 = jnp.float32
DP = ("x", "y", "core")


def dot(a, b, dims):
    return lax.dot_general(a, b, (dims, ((), ())), preferred_element_type=F32)


def segments_of(ends, shape, dim):
    places = lax.broadcasted_iota(jnp.int32, shape, dim)
    passed = jnp.zeros(shape, jnp.int32)
    for end in ends:
        passed = passed + (places >= end).astype(jnp.int32)
    return jnp.where(passed == len(ends), -1, passed)


def masks(seg_column, seg_row):
    length = seg_column.shape[0]
    square = (length, length)
    same = seg_column == seg_row
    earlier = lax.broadcasted_iota(jnp.int32, square, 1) <= lax.broadcasted_iota(jnp.int32, square, 0)
    allowed = same & earlier & (seg_column >= 0)
    counts = jnp.sum(same.astype(F32), axis=1, keepdims=True)
    return allowed, counts


def forward(values, queries, key_rows, allowed, counts):
    width = values.shape[1]
    head_dim = width // HEADS
    scale = 1.0 / math.sqrt(head_dim)
    scores, sigmas, weights, mixed = [], [], [], []
    for h in range(HEADS):
        cols = slice(h * head_dim, (h + 1) * head_dim)
        s = dot(queries[:, cols], key_rows[:, cols], ((1,), (1,))) * scale
        sigma = jax.nn.sigmoid(s)
        w = (jnp.where(allowed, s * sigma, 0.0) / counts).astype(BF16)
        scores.append(s)
        sigmas.append(sigma)
        weights.append(w)
        mixed.append(dot(w, values[:, cols], ((1,), (0,))))
    mixed = jnp.concatenate(mixed, axis=1)
    centered = mixed - jnp.mean(mixed, axis=1, keepdims=True)
    inverse = lax.rsqrt(jnp.mean(centered * centered, axis=1, keepdims=True) + EPS)
    return scores, sigmas, weights, centered * inverse, inverse


def backward(gate, values, queries, key_rows, grad_y, allowed, counts, put):
    width = values.shape[1]
    head_dim = width // HEADS
    scale = 1.0 / math.sqrt(head_dim)
    scores, sigmas, weights, normed, inverse = forward(values, queries, key_rows, allowed, counts)
    put(0, slice(0, width), grad_y * normed)
    grad_normed = grad_y * gate.astype(F32)
    grad_mixed = inverse * (
        grad_normed
        - jnp.mean(grad_normed, axis=1, keepdims=True)
        - normed * jnp.mean(grad_normed * normed, axis=1, keepdims=True)
    )
    grad_mixed = grad_mixed.astype(BF16)
    factor = scale / counts
    for h in range(HEADS):
        cols = slice(h * head_dim, (h + 1) * head_dim)
        s, sigma = scores[h], sigmas[h]
        grad_weights = dot(grad_mixed[:, cols], values[:, cols], ((1,), (1,)))
        put(1, cols, dot(weights[h], grad_mixed[:, cols], ((0,), (0,))))
        slope = sigma * (1.0 + s * (1.0 - sigma))
        grad_scores = (jnp.where(allowed, grad_weights * slope, 0.0) * factor).astype(BF16)
        put(2, cols, dot(grad_scores, key_rows[:, cols], ((1,), (0,))))
        put(3, cols, dot(grad_scores, queries[:, cols], ((0,), (0,))))


def shares(row_groups, col_groups, share_cols):
    for r in range(row_groups):
        for c in range(col_groups):
            yield r * col_groups + c, r * GROUP_ROWS, c * share_cols


def pack_kernel(keep, x_ref, g_ref, out_ref, block_ref, sems):
    width, joint = x_ref.shape[1], block_ref.shape[1]
    moved = block_ref.shape[0]
    share_cols = out_ref.shape[2]
    rows = pl.ds(keep, moved)
    from_x = pltpu.make_async_copy(x_ref.at[rows], block_ref.at[:, pl.ds(0, width)], sems.at[0])
    from_g = pltpu.make_async_copy(g_ref.at[rows], block_ref.at[:, pl.ds(width, joint - width)], sems.at[1])
    from_x.start()
    from_g.start()
    from_x.wait()
    from_g.wait()
    for share, row, start in shares(moved // GROUP_ROWS, joint // share_cols, share_cols):
        out_ref[share] = block_ref[pl.ds(row, GROUP_ROWS), pl.ds(start, share_cols)]


def term_kernel(keep, core_ref, lengths_ref, x_ref, g_ref, seg_col_ref, seg_row_ref, mine_ref, other_ref, y_ref):
    width = g_ref.shape[1]
    rows_all = x_ref.shape[0]

    def rows_of(rows, allowed, counts):
        values, queries, key_rows = (x_ref[rows, pl.ds((1 + i) * width, width)] for i in range(3))
        normed = forward(values, queries, key_rows, allowed, counts)[3]
        y_ref[rows, :] = (normed * x_ref[rows, pl.ds(0, width)].astype(F32)).astype(BF16)

    moved = rows_all - keep
    total, ends = 0, []
    for i in range(lengths_ref.shape[1]):
        total = total + lengths_ref[0, i]
        ends.append(total)
    rows_of(pl.ds(keep, moved), *masks(segments_of(ends, (moved, 1), 0), segments_of(ends, (1, moved), 1)))
    rows_of(pl.ds(0, keep), *masks(seg_col_ref[...], seg_row_ref[...]))
    half_cols = mine_ref.shape[1]
    core = core_ref[0]
    for half, term_ref in ((core, mine_ref), (1 - core, other_ref)):
        for b in range(0, half_cols, 256):
            start = pl.multiple_of(half * half_cols + b, 256)
            found = dot(g_ref[...], y_ref[:, pl.ds(start, 256)], ((0,), (0,)))
            term_ref[:, pl.ds(b, 256)] = found.astype(BF16)


def back_kernel(keep, lengths_ref, x_ref, g_ref, came_ref, w_ref, seg_col_ref, seg_row_ref, out_ref, block_ref):
    width = g_ref.shape[1]
    moved, joint = block_ref.shape
    share_cols = came_ref.shape[2]
    for share, row, start in shares(moved // GROUP_ROWS, joint // share_cols, share_cols):
        block_ref[pl.ds(row, GROUP_ROWS), pl.ds(start, share_cols)] = came_ref[share]

    def put_in(rows):
        def put(part, cols, found):
            out_ref[rows, pl.ds(part * width + cols.start, cols.stop - cols.start)] = found.astype(BF16)

        return put

    total, ends = 0, []
    for i in range(lengths_ref.shape[1]):
        total = total + lengths_ref[0, i]
        ends.append(total)
    kept_grad_y = dot(g_ref[pl.ds(0, keep), :], w_ref[...], ((1,), (0,)))
    parts = [x_ref[pl.ds(0, keep), pl.ds(i * width, width)] for i in range(4)]
    backward(*parts, kept_grad_y, *masks(seg_col_ref[...], seg_row_ref[...]), put_in(pl.ds(0, keep)))
    *parts, grads = [block_ref[:, pl.ds(i * width, width)] for i in range(5)]
    grad_y = dot(grads, w_ref[...], ((1,), (0,)))
    backward(
        *parts,
        grad_y,
        *masks(segments_of(ends, (moved, 1), 0), segments_of(ends, (1, moved), 1)),
        put_in(pl.ds(keep, moved)),
    )


VMEM = pl.BlockSpec(memory_space=pltpu.VMEM)
HBM = pl.BlockSpec(memory_space=pltpu.HBM)
SMEM = pl.BlockSpec(memory_space=pltpu.SMEM)
PARAMS = pltpu.CompilerParams(vmem_limit_bytes=24 * 2**20)


def cost(flops, nbytes):
    return pl.CostEstimate(flops=flops, bytes_accessed=nbytes, transcendentals=0)


def permuted(value, axis, target):
    size = lax.axis_size(axis)
    return lax.ppermute(value, axis, [(i, target(i)) for i in range(size)])


def pick(value, index, dim=0):
    return lax.dynamic_index_in_dim(value, index, dim, keepdims=False)


def added(*values):
    return functools.reduce(jnp.add, [value.astype(F32) for value in values])


def halving_round(value, axis, bit):
    pairs = value.reshape((value.shape[0] // 2, 2) + value.shape[1:])
    mine = (lax.axis_index(axis) >> bit) & 1
    came = permuted(pick(pairs, 1 - mine, 1), axis, lambda i: i ^ (1 << bit))
    return added(pick(pairs, mine, 1), came).astype(BF16)


def direct_round(value, axis, stride):
    size, outer = lax.axis_size(axis), value.shape[0]
    high = lax.axis_index(axis) // stride
    came = [
        permuted(pick(value, (high + step) & (outer - 1)), axis, lambda i, step=step: (i + step * stride) % size)
        for step in range(1, outer)
    ]
    return added(pick(value, high), *came)


def exchange(value, axes=DP):
    return lax.all_to_all(value, axes, split_axis=0, concat_axis=0, tiled=True)


def local(uvqk, grad_out, w_out, kept_segments, moved_lengths, dest_device):
    keep = kept_segments.shape[1]
    rows, width = grad_out.shape
    moved = rows - keep
    n_x, n_y, n_core, n_z = (lax.axis_size(a) for a in ("x", "y", "core", "z"))
    groups = n_x * n_y * n_core
    dp_index, z_index = lax.axis_index(DP), lax.axis_index("z")
    indices = jnp.arange(groups, dtype=jnp.int32)
    seg_col, seg_row = kept_segments.reshape(keep, 1), kept_segments

    w_all = lax.all_gather(w_out, "z", axis=0, tiled=True)
    share_cols = 5 * width * (moved // GROUP_ROWS) // groups
    block = pl.pallas_call(
        functools.partial(pack_kernel, keep),
        out_shape=jax.ShapeDtypeStruct((groups, GROUP_ROWS, share_cols), BF16),
        in_specs=[HBM, HBM],
        out_specs=VMEM,
        scratch_shapes=[pltpu.VMEM((moved, 5 * width), BF16), pltpu.SemaphoreType.DMA((2,))],
        compiler_params=pltpu.CompilerParams(vmem_limit_bytes=60 * 2**20),
        cost_estimate=cost(0, 8 * width),
        name="pack",
    )(uvqk, grad_out)
    uvqk, grad_out, dest_device, block = lax.optimization_barrier((uvqk, grad_out, dest_device, block))
    block = exchange(block)

    source_of = jnp.sum(jnp.where(dest_device[None, :] == indices[:, None], indices[None, :], 0), axis=1)
    own_source = jnp.sum(jnp.where(dest_device == dp_index, indices, 0))
    own_lengths = lax.dynamic_slice_in_dim(moved_lengths, dp_index * n_z + z_index, 1, 0)
    recv_lengths = lax.dynamic_slice_in_dim(moved_lengths, own_source * n_z + z_index, 1, 0)
    half_cols = width // n_core
    core_half = jax.ShapeDtypeStruct((width, half_cols), BF16)
    mine, other = pl.pallas_call(
        functools.partial(term_kernel, keep),
        out_shape=(core_half, core_half),
        in_specs=[SMEM, SMEM, VMEM, VMEM, VMEM, VMEM],
        out_specs=(VMEM, VMEM),
        scratch_shapes=[pltpu.VMEM((rows, width), BF16)],
        compiler_params=PARAMS,
        cost_estimate=cost(0, 8 * width),
        name="term",
    )(lax.axis_index("core").reshape(1), own_lengths, uvqk, grad_out, seg_col, seg_row)
    part = added(mine, permuted(other, "core", lambda i: i ^ 1)).astype(BF16)
    own_rows = width // n_z
    part = halving_round(part.reshape(n_z, own_rows, half_cols), "z", 0)
    block = lax.optimization_barrier((block, part))[0]
    block = exchange(block[source_of])
    stride = 2
    if part.shape[0] > 4:
        part, stride = halving_round(part, "z", 1), 4
    part = direct_round(part, "z", stride)

    part = lax.optimization_barrier((part, block))[0]
    col_blocks = half_cols // 128
    row_blocks = n_x * n_y // col_blocks
    tile_rows = own_rows // row_blocks
    part = part.astype(BF16).reshape(row_blocks, tile_rows, col_blocks, 128).transpose(0, 2, 1, 3)
    part = exchange(part.reshape(n_x * n_y, tile_rows, 128), ("x", "y"))
    part = (jnp.sum(part.astype(F32), axis=0) * (1.0 / (groups * n_z))).astype(BF16)
    spread = exchange(jnp.broadcast_to(part[None], (groups,) + part.shape)).astype(F32)
    spread = spread.reshape(row_blocks, col_blocks, n_core, tile_rows, 128)
    grad_weight = spread.transpose(0, 3, 2, 1, 4).reshape(own_rows, width)

    grad_rows = pl.pallas_call(
        functools.partial(back_kernel, keep),
        out_shape=jax.ShapeDtypeStruct(uvqk.shape, BF16),
        in_specs=[SMEM] + [VMEM] * 6,
        out_specs=VMEM,
        scratch_shapes=[pltpu.VMEM((moved, 5 * width), BF16)],
        compiler_params=PARAMS,
        cost_estimate=cost(8 * rows * width * width, 8 * width * width),
        name="back",
    )(recv_lengths, uvqk, grad_out, block, w_all, seg_col, seg_row)
    return grad_rows, grad_weight


def fine_mesh(mesh):
    n_dp, n_z = mesh.devices.shape
    n_core = 2
    n_x = min(4, n_dp // 4)
    shape = (n_x, n_dp // (n_x * n_core), n_core, n_z)
    return Mesh(mesh.devices.reshape(shape), ("x", "y", "core", "z"))


def solution(mesh):
    everyone = P(("x", "y", "core", "z"), None)
    placed = (everyone, everyone, P("z", None), everyone, P(), P())
    return jax.shard_map(
        local,
        mesh=fine_mesh(mesh),
        in_specs=placed,
        out_specs=(everyone, P("z", None)),
        check_vma=False,
    )
```

```python
import functools
import math

import jax
import jax.numpy as jnp
from jax import lax
from jax.experimental import pallas as pl
from jax.experimental.pallas import tpu as pltpu
from jax.sharding import Mesh
from jax.sharding import PartitionSpec as P

HEADS = 4
EPS = 1e-05
GROUP_ROWS = 16
BF16 = jnp.bfloat16
F32 = jnp.float32
DP = ("x", "y", "core")


def dot(a, b, dims):
    return lax.dot_general(a, b, (dims, ((), ())), preferred_element_type=F32)


def segments_of(ends, shape, dim):
    places = lax.broadcasted_iota(jnp.int32, shape, dim)
    passed = jnp.zeros(shape, jnp.int32)
    for end in ends:
        passed = passed + (places >= end).astype(jnp.int32)
    return jnp.where(passed == len(ends), -1, passed)


def masks(seg_column, seg_row):
    length = seg_column.shape[0]
    square = (length, length)
    same = seg_column == seg_row
    earlier = lax.broadcasted_iota(jnp.int32, square, 1) <= lax.broadcasted_iota(jnp.int32, square, 0)
    allowed = same & earlier & (seg_column >= 0)
    counts = jnp.sum(same.astype(F32), axis=1, keepdims=True)
    return allowed, counts


def forward(values, queries, key_rows, allowed, counts):
    width = values.shape[1]
    head_dim = width // HEADS
    scale = 1.0 / math.sqrt(head_dim)
    scores, sigmas, weights, mixed = [], [], [], []
    for h in range(HEADS):
        cols = slice(h * head_dim, (h + 1) * head_dim)
        s = dot(queries[:, cols], key_rows[:, cols], ((1,), (1,))) * scale
        sigma = jax.nn.sigmoid(s)
        w = (jnp.where(allowed, s * sigma, 0.0) / counts).astype(BF16)
        scores.append(s)
        sigmas.append(sigma)
        weights.append(w)
        mixed.append(dot(w, values[:, cols], ((1,), (0,))))
    mixed = jnp.concatenate(mixed, axis=1)
    centered = mixed - jnp.mean(mixed, axis=1, keepdims=True)
    inverse = lax.rsqrt(jnp.mean(centered * centered, axis=1, keepdims=True) + EPS)
    return scores, sigmas, weights, centered * inverse, inverse


def backward(gate, values, queries, key_rows, grad_y, allowed, counts, put):
    width = values.shape[1]
    head_dim = width // HEADS
    scale = 1.0 / math.sqrt(head_dim)
    scores, sigmas, weights, normed, inverse = forward(values, queries, key_rows, allowed, counts)
    put(0, slice(0, width), grad_y * normed)
    grad_normed = grad_y * gate.astype(F32)
    grad_mixed = inverse * (
        grad_normed
        - jnp.mean(grad_normed, axis=1, keepdims=True)
        - normed * jnp.mean(grad_normed * normed, axis=1, keepdims=True)
    )
    grad_mixed = grad_mixed.astype(BF16)
    factor = scale / counts
    for h in range(HEADS):
        cols = slice(h * head_dim, (h + 1) * head_dim)
        s, sigma = scores[h], sigmas[h]
        grad_weights = dot(grad_mixed[:, cols], values[:, cols], ((1,), (1,)))
        put(1, cols, dot(weights[h], grad_mixed[:, cols], ((0,), (0,))))
        slope = sigma * (1.0 + s * (1.0 - sigma))
        grad_scores = (jnp.where(allowed, grad_weights * slope, 0.0) * factor).astype(BF16)
        put(2, cols, dot(grad_scores, key_rows[:, cols], ((1,), (0,))))
        put(3, cols, dot(grad_scores, queries[:, cols], ((0,), (0,))))


def shares(row_groups, col_groups, share_cols):
    for r in range(row_groups):
        for c in range(col_groups):
            yield r * col_groups + c, r * GROUP_ROWS, c * share_cols


def pack_kernel(keep, x_ref, g_ref, out_ref, block_ref, sems):
    width, joint = x_ref.shape[1], block_ref.shape[1]
    moved = block_ref.shape[0]
    share_cols = out_ref.shape[2]
    rows = pl.ds(keep, moved)
    from_x = pltpu.make_async_copy(x_ref.at[rows], block_ref.at[:, pl.ds(0, width)], sems.at[0])
    from_g = pltpu.make_async_copy(g_ref.at[rows], block_ref.at[:, pl.ds(width, joint - width)], sems.at[1])
    from_x.start()
    from_g.start()
    from_x.wait()
    from_g.wait()
    for share, row, start in shares(moved // GROUP_ROWS, joint // share_cols, share_cols):
        out_ref[share] = block_ref[pl.ds(row, GROUP_ROWS), pl.ds(start, share_cols)]


def term_kernel(keep, core_ref, lengths_ref, x_ref, g_ref, seg_col_ref, seg_row_ref, mine_ref, other_ref, y_ref):
    width = g_ref.shape[1]
    rows_all = x_ref.shape[0]

    def rows_of(rows, allowed, counts):
        values, queries, key_rows = (x_ref[rows, pl.ds((1 + i) * width, width)] for i in range(3))
        normed = forward(values, queries, key_rows, allowed, counts)[3]
        y_ref[rows, :] = (normed * x_ref[rows, pl.ds(0, width)].astype(F32)).astype(BF16)

    moved = rows_all - keep
    total, ends = 0, []
    for i in range(lengths_ref.shape[1]):
        total = total + lengths_ref[0, i]
        ends.append(total)
    rows_of(pl.ds(keep, moved), *masks(segments_of(ends, (moved, 1), 0), segments_of(ends, (1, moved), 1)))
    rows_of(pl.ds(0, keep), *masks(seg_col_ref[...], seg_row_ref[...]))
    blocks, _, block_cols = mine_ref.shape
    joined = max(1, 256 // block_cols)
    core = core_ref[0]
    for half, term_ref in ((core, mine_ref), (1 - core, other_ref)):
        for b in range(0, blocks, joined):
            start = pl.multiple_of((half * blocks + b) * block_cols, 128)
            found = dot(g_ref[...], y_ref[:, pl.ds(start, joined * block_cols)], ((0,), (0,)))
            for i in range(joined):
                term_ref[b + i] = found[:, i * block_cols : (i + 1) * block_cols].astype(BF16)


def back_kernel(keep, lengths_ref, x_ref, g_ref, came_ref, w_ref, seg_col_ref, seg_row_ref, out_ref, block_ref):
    width = g_ref.shape[1]
    moved, joint = block_ref.shape
    share_cols = came_ref.shape[2]
    for share, row, start in shares(moved // GROUP_ROWS, joint // share_cols, share_cols):
        block_ref[pl.ds(row, GROUP_ROWS), pl.ds(start, share_cols)] = came_ref[share]

    def put_in(rows):
        def put(part, cols, found):
            out_ref[rows, pl.ds(part * width + cols.start, cols.stop - cols.start)] = found.astype(BF16)

        return put

    total, ends = 0, []
    for i in range(lengths_ref.shape[1]):
        total = total + lengths_ref[0, i]
        ends.append(total)
    kept_grad_y = dot(g_ref[pl.ds(0, keep), :], w_ref[...], ((1,), (0,)))
    parts = [x_ref[pl.ds(0, keep), pl.ds(i * width, width)] for i in range(4)]
    backward(*parts, kept_grad_y, *masks(seg_col_ref[...], seg_row_ref[...]), put_in(pl.ds(0, keep)))
    *parts, grads = [block_ref[:, pl.ds(i * width, width)] for i in range(5)]
    grad_y = dot(grads, w_ref[...], ((1,), (0,)))
    backward(
        *parts,
        grad_y,
        *masks(segments_of(ends, (moved, 1), 0), segments_of(ends, (1, moved), 1)),
        put_in(pl.ds(keep, moved)),
    )


VMEM = pl.BlockSpec(memory_space=pltpu.VMEM)
HBM = pl.BlockSpec(memory_space=pltpu.HBM)
SMEM = pl.BlockSpec(memory_space=pltpu.SMEM)
PARAMS = pltpu.CompilerParams(vmem_limit_bytes=24 * 2**20)


def cost(flops, nbytes):
    return pl.CostEstimate(flops=flops, bytes_accessed=nbytes, transcendentals=0)


def permuted(value, axis, target):
    size = lax.axis_size(axis)
    return lax.ppermute(value, axis, [(i, target(i)) for i in range(size)])


def pick(value, index, dim=0):
    return lax.dynamic_index_in_dim(value, index, dim, keepdims=False)


def added(*values):
    return functools.reduce(jnp.add, [value.astype(F32) for value in values])


def scatter_sum(value, axis):
    size, me = lax.axis_size(axis), lax.axis_index(axis)
    came = [
        permuted(pick(value, (me + step) & (size - 1)), axis, lambda i, step=step: (i + step) % size)
        for step in range(1, size)
    ]
    return added(pick(value, me), *came).astype(BF16)


def ring_of_rings_sum(value, axis, inner):
    size, me = lax.axis_size(axis), lax.axis_index(axis)
    outer = size // inner
    value = value.reshape((outer, inner) + value.shape[1:])
    low, high = me & (inner - 1), me >> (inner.bit_length() - 1)
    came = [
        permuted(
            pick(value, (low + step) & (inner - 1), 1),
            axis,
            lambda i, step=step: i // inner * inner + (i + step) % inner,
        )
        for step in range(1, inner)
    ]
    value = added(pick(value, low, 1), *came).astype(BF16)
    came = [
        permuted(pick(value, (high + step) & (outer - 1)), axis, lambda i, step=step: (i + step * inner) % size)
        for step in range(1, outer)
    ]
    return added(pick(value, high), *came)


def exchange(value, axes=DP):
    return lax.all_to_all(value, axes, split_axis=0, concat_axis=0, tiled=True)


def local(uvqk, grad_out, w_out, kept_segments, moved_lengths, dest_device):
    keep = kept_segments.shape[1]
    rows, width = grad_out.shape
    moved = rows - keep
    n_x, n_y, n_core, n_z = (lax.axis_size(a) for a in ("x", "y", "core", "z"))
    groups = n_x * n_y * n_core
    dp_index, z_index = lax.axis_index(DP), lax.axis_index("z")
    indices = jnp.arange(groups, dtype=jnp.int32)
    seg_col, seg_row = kept_segments.reshape(keep, 1), kept_segments

    w_all = lax.all_gather(w_out, "z", axis=0, tiled=True)
    share_cols = 5 * width * (moved // GROUP_ROWS) // groups
    block = pl.pallas_call(
        functools.partial(pack_kernel, keep),
        out_shape=jax.ShapeDtypeStruct((groups, GROUP_ROWS, share_cols), BF16),
        in_specs=[HBM, HBM],
        out_specs=VMEM,
        scratch_shapes=[pltpu.VMEM((moved, 5 * width), BF16), pltpu.SemaphoreType.DMA((2,))],
        compiler_params=pltpu.CompilerParams(vmem_limit_bytes=60 * 2**20),
        cost_estimate=cost(0, 8 * width),
        name="pack",
    )(uvqk, grad_out)
    uvqk, grad_out, dest_device, block = lax.optimization_barrier((uvqk, grad_out, dest_device, block))
    block = exchange(block)

    source_of = jnp.sum(jnp.where(dest_device[None, :] == indices[:, None], indices[None, :], 0), axis=1)
    own_source = jnp.sum(jnp.where(dest_device == dp_index, indices, 0))
    own_lengths = lax.dynamic_slice_in_dim(moved_lengths, dp_index * n_z + z_index, 1, 0)
    recv_lengths = lax.dynamic_slice_in_dim(moved_lengths, own_source * n_z + z_index, 1, 0)
    block_cols = width // (n_core * n_x)
    core_half = jax.ShapeDtypeStruct((n_x, width, block_cols), BF16)
    mine, other = pl.pallas_call(
        functools.partial(term_kernel, keep),
        out_shape=(core_half, core_half),
        in_specs=[SMEM, SMEM, VMEM, VMEM, VMEM, VMEM],
        out_specs=(VMEM, VMEM),
        scratch_shapes=[pltpu.VMEM((rows, width), BF16)],
        compiler_params=PARAMS,
        cost_estimate=cost(0, 8 * width),
        name="term",
    )(lax.axis_index("core").reshape(1), own_lengths, uvqk, grad_out, seg_col, seg_row)
    part = added(mine, permuted(other, "core", lambda i: i ^ 1)).astype(BF16)
    part = scatter_sum(part, "x")
    own_rows = width // n_z
    part, block = lax.optimization_barrier((part, block))
    block = exchange(block[source_of])
    own_rows = width // n_z
    part = ring_of_rings_sum(part.reshape(n_z, own_rows, block_cols), "z", min(4, n_z)).astype(BF16)
    part = lax.optimization_barrier((part, block))[0]
    part = exchange(jnp.broadcast_to(part[None], (n_y,) + part.shape), "y")
    part = (jnp.sum(part.astype(F32), axis=0) * (1.0 / (groups * n_z))).astype(BF16)
    spread = exchange(jnp.broadcast_to(part[None], (n_x * n_core,) + part.shape), ("x", "core"))
    spread = spread.reshape(n_x, n_core, own_rows, block_cols).transpose(2, 1, 0, 3)
    grad_weight = spread.reshape(own_rows, width).astype(F32)

    grad_rows = pl.pallas_call(
        functools.partial(back_kernel, keep),
        out_shape=jax.ShapeDtypeStruct(uvqk.shape, BF16),
        in_specs=[SMEM] + [VMEM] * 6,
        out_specs=VMEM,
        scratch_shapes=[pltpu.VMEM((moved, 5 * width), BF16)],
        compiler_params=PARAMS,
        cost_estimate=cost(8 * rows * width * width, 8 * width * width),
        name="back",
    )(recv_lengths, uvqk, grad_out, block, w_all, seg_col, seg_row)
    return grad_rows, grad_weight


def fine_mesh(mesh):
    n_dp, n_z = mesh.devices.shape
    n_core = 2
    n_x = min(4, n_dp // 4)
    shape = (n_x, n_dp // (n_x * n_core), n_core, n_z)
    return Mesh(mesh.devices.reshape(shape), ("x", "y", "core", "z"))


def solution(mesh):
    everyone = P(("x", "y", "core", "z"), None)
    placed = (everyone, everyone, P("z", None), everyone, P(), P())
    return jax.shard_map(
        local,
        mesh=fine_mesh(mesh),
        in_specs=placed,
        out_specs=(everyone, P("z", None)),
        check_vma=False,
    )
```

```python
import functools
import math

import jax
import jax.numpy as jnp
from jax import lax
from jax.experimental import pallas as pl
from jax.experimental.pallas import tpu as pltpu
from jax.sharding import Mesh
from jax.sharding import PartitionSpec as P

HEADS = 4
EPS = 1e-05
GROUP_ROWS = 16
BF16 = jnp.bfloat16
F32 = jnp.float32
DP = ("x", "y", "core")


def dot(a, b, dims):
    return lax.dot_general(a, b, (dims, ((), ())), preferred_element_type=F32)


def segments_of(ends, shape, dim):
    places = lax.broadcasted_iota(jnp.int32, shape, dim)
    passed = jnp.zeros(shape, jnp.int32)
    for end in ends:
        passed = passed + (places >= end).astype(jnp.int32)
    return jnp.where(passed == len(ends), -1, passed)


def masks(seg_column, seg_row):
    length = seg_column.shape[0]
    square = (length, length)
    same = seg_column == seg_row
    earlier = lax.broadcasted_iota(jnp.int32, square, 1) <= lax.broadcasted_iota(jnp.int32, square, 0)
    allowed = same & earlier & (seg_column >= 0)
    counts = jnp.sum(same.astype(F32), axis=1, keepdims=True)
    return allowed, counts


def forward(values, queries, key_rows, allowed, counts):
    width = values.shape[1]
    head_dim = width // HEADS
    scale = 1.0 / math.sqrt(head_dim)
    scores, sigmas, weights, mixed = [], [], [], []
    for h in range(HEADS):
        cols = slice(h * head_dim, (h + 1) * head_dim)
        s = dot(queries[:, cols], key_rows[:, cols], ((1,), (1,))) * scale
        sigma = jax.nn.sigmoid(s)
        w = (jnp.where(allowed, s * sigma, 0.0) / counts).astype(BF16)
        scores.append(s)
        sigmas.append(sigma)
        weights.append(w)
        mixed.append(dot(w, values[:, cols], ((1,), (0,))))
    mixed = jnp.concatenate(mixed, axis=1)
    centered = mixed - jnp.mean(mixed, axis=1, keepdims=True)
    inverse = lax.rsqrt(jnp.mean(centered * centered, axis=1, keepdims=True) + EPS)
    return scores, sigmas, weights, centered * inverse, inverse


def backward(gate, values, queries, key_rows, grad_y, allowed, counts, put):
    width = values.shape[1]
    head_dim = width // HEADS
    scale = 1.0 / math.sqrt(head_dim)
    scores, sigmas, weights, normed, inverse = forward(values, queries, key_rows, allowed, counts)
    put(0, slice(0, width), grad_y * normed)
    grad_normed = grad_y * gate.astype(F32)
    grad_mixed = inverse * (
        grad_normed
        - jnp.mean(grad_normed, axis=1, keepdims=True)
        - normed * jnp.mean(grad_normed * normed, axis=1, keepdims=True)
    )
    grad_mixed = grad_mixed.astype(BF16)
    factor = scale / counts
    for h in range(HEADS):
        cols = slice(h * head_dim, (h + 1) * head_dim)
        s, sigma = scores[h], sigmas[h]
        grad_weights = dot(grad_mixed[:, cols], values[:, cols], ((1,), (1,)))
        put(1, cols, dot(weights[h], grad_mixed[:, cols], ((0,), (0,))))
        slope = sigma * (1.0 + s * (1.0 - sigma))
        grad_scores = (jnp.where(allowed, grad_weights * slope, 0.0) * factor).astype(BF16)
        put(2, cols, dot(grad_scores, key_rows[:, cols], ((1,), (0,))))
        put(3, cols, dot(grad_scores, queries[:, cols], ((0,), (0,))))


def shares(row_groups, col_groups, share_cols):
    for r in range(row_groups):
        for c in range(col_groups):
            yield r * col_groups + c, r * GROUP_ROWS, c * share_cols


def pack_kernel(keep, x_ref, g_ref, out_ref, block_ref, sems):
    width, joint = x_ref.shape[1], block_ref.shape[1]
    moved = block_ref.shape[0]
    share_cols = out_ref.shape[2]
    rows = pl.ds(keep, moved)
    from_x = pltpu.make_async_copy(x_ref.at[rows], block_ref.at[:, pl.ds(0, width)], sems.at[0])
    from_g = pltpu.make_async_copy(g_ref.at[rows], block_ref.at[:, pl.ds(width, joint - width)], sems.at[1])
    from_x.start()
    from_g.start()
    from_x.wait()
    from_g.wait()
    for share, row, start in shares(moved // GROUP_ROWS, joint // share_cols, share_cols):
        out_ref[share] = block_ref[pl.ds(row, GROUP_ROWS), pl.ds(start, share_cols)]


def term_kernel(keep, core_ref, lengths_ref, x_ref, g_ref, seg_col_ref, seg_row_ref, mine_ref, other_ref, y_ref):
    width = g_ref.shape[1]
    rows_all = x_ref.shape[0]

    def rows_of(rows, allowed, counts):
        values, queries, key_rows = (x_ref[rows, pl.ds((1 + i) * width, width)] for i in range(3))
        normed = forward(values, queries, key_rows, allowed, counts)[3]
        y_ref[rows, :] = (normed * x_ref[rows, pl.ds(0, width)].astype(F32)).astype(BF16)

    moved = rows_all - keep
    total, ends = 0, []
    for i in range(lengths_ref.shape[1]):
        total = total + lengths_ref[0, i]
        ends.append(total)
    rows_of(pl.ds(keep, moved), *masks(segments_of(ends, (moved, 1), 0), segments_of(ends, (1, moved), 1)))
    rows_of(pl.ds(0, keep), *masks(seg_col_ref[...], seg_row_ref[...]))
    blocks, _, block_cols = mine_ref.shape
    joined = max(1, 256 // block_cols)
    core = core_ref[0]
    for half, term_ref in ((core, mine_ref), (1 - core, other_ref)):
        for b in range(0, blocks, joined):
            start = pl.multiple_of((half * blocks + b) * block_cols, 128)
            found = dot(g_ref[...], y_ref[:, pl.ds(start, joined * block_cols)], ((0,), (0,)))
            for i in range(joined):
                term_ref[b + i] = found[:, i * block_cols : (i + 1) * block_cols].astype(BF16)


def back_kernel(keep, lengths_ref, x_ref, g_ref, came_ref, w_ref, seg_col_ref, seg_row_ref, out_ref, block_ref):
    width = g_ref.shape[1]
    moved, joint = block_ref.shape
    share_cols = came_ref.shape[2]
    for share, row, start in shares(moved // GROUP_ROWS, joint // share_cols, share_cols):
        block_ref[pl.ds(row, GROUP_ROWS), pl.ds(start, share_cols)] = came_ref[share]

    def put_in(rows):
        def put(part, cols, found):
            out_ref[rows, pl.ds(part * width + cols.start, cols.stop - cols.start)] = found.astype(BF16)

        return put

    total, ends = 0, []
    for i in range(lengths_ref.shape[1]):
        total = total + lengths_ref[0, i]
        ends.append(total)
    kept_grad_y = dot(g_ref[pl.ds(0, keep), :], w_ref[...], ((1,), (0,)))
    parts = [x_ref[pl.ds(0, keep), pl.ds(i * width, width)] for i in range(4)]
    backward(*parts, kept_grad_y, *masks(seg_col_ref[...], seg_row_ref[...]), put_in(pl.ds(0, keep)))
    *parts, grads = [block_ref[:, pl.ds(i * width, width)] for i in range(5)]
    grad_y = dot(grads, w_ref[...], ((1,), (0,)))
    backward(
        *parts,
        grad_y,
        *masks(segments_of(ends, (moved, 1), 0), segments_of(ends, (1, moved), 1)),
        put_in(pl.ds(keep, moved)),
    )


VMEM = pl.BlockSpec(memory_space=pltpu.VMEM)
HBM = pl.BlockSpec(memory_space=pltpu.HBM)
SMEM = pl.BlockSpec(memory_space=pltpu.SMEM)
PARAMS = pltpu.CompilerParams(vmem_limit_bytes=24 * 2**20)


def cost(flops, nbytes):
    return pl.CostEstimate(flops=flops, bytes_accessed=nbytes, transcendentals=0)


def permuted(value, axis, target):
    size = lax.axis_size(axis)
    return lax.ppermute(value, axis, [(i, target(i)) for i in range(size)])


def pick(value, index, dim=0):
    return lax.dynamic_index_in_dim(value, index, dim, keepdims=False)


def added(*values):
    return functools.reduce(jnp.add, [value.astype(F32) for value in values])


def scatter_sum(value, axis):
    size, me = lax.axis_size(axis), lax.axis_index(axis)
    came = [
        permuted(pick(value, (me + step) & (size - 1)), axis, lambda i, step=step: (i + step) % size)
        for step in range(1, size)
    ]
    return added(pick(value, me), *came).astype(BF16)


def ring_of_rings_sum(value, axis, inner):
    size, me = lax.axis_size(axis), lax.axis_index(axis)
    outer = size // inner
    value = value.reshape((outer, inner) + value.shape[1:])
    low, high = me & (inner - 1), me >> (inner.bit_length() - 1)
    came = [
        permuted(
            pick(value, (low + step) & (inner - 1), 1),
            axis,
            lambda i, step=step: i // inner * inner + (i + step) % inner,
        )
        for step in range(1, inner)
    ]
    value = added(pick(value, low, 1), *came).astype(BF16)
    came = [
        permuted(pick(value, (high + step) & (outer - 1)), axis, lambda i, step=step: (i + step * inner) % size)
        for step in range(1, outer)
    ]
    return added(pick(value, high), *came)


def exchange(value, axes=DP):
    return lax.all_to_all(value, axes, split_axis=0, concat_axis=0, tiled=True)


def local(uvqk, grad_out, w_out, kept_segments, moved_lengths, dest_device):
    keep = kept_segments.shape[1]
    rows, width = grad_out.shape
    moved = rows - keep
    n_x, n_y, n_core, n_z = (lax.axis_size(a) for a in ("x", "y", "core", "z"))
    groups = n_x * n_y * n_core
    dp_index, z_index = lax.axis_index(DP), lax.axis_index("z")
    indices = jnp.arange(groups, dtype=jnp.int32)
    seg_col, seg_row = kept_segments.reshape(keep, 1), kept_segments

    w_all = lax.all_gather(w_out, "z", axis=0, tiled=True)
    share_cols = 5 * width * (moved // GROUP_ROWS) // groups
    block = pl.pallas_call(
        functools.partial(pack_kernel, keep),
        out_shape=jax.ShapeDtypeStruct((groups, GROUP_ROWS, share_cols), BF16),
        in_specs=[HBM, HBM],
        out_specs=VMEM,
        scratch_shapes=[pltpu.VMEM((moved, 5 * width), BF16), pltpu.SemaphoreType.DMA((2,))],
        compiler_params=pltpu.CompilerParams(vmem_limit_bytes=60 * 2**20),
        cost_estimate=cost(0, 8 * width),
        name="pack",
    )(uvqk, grad_out)
    uvqk, grad_out, dest_device, block = lax.optimization_barrier((uvqk, grad_out, dest_device, block))
    block = exchange(block)

    source_of = jnp.sum(jnp.where(dest_device[None, :] == indices[:, None], indices[None, :], 0), axis=1)
    own_source = jnp.sum(jnp.where(dest_device == dp_index, indices, 0))
    own_lengths = lax.dynamic_slice_in_dim(moved_lengths, dp_index * n_z + z_index, 1, 0)
    recv_lengths = lax.dynamic_slice_in_dim(moved_lengths, own_source * n_z + z_index, 1, 0)
    block_cols = width // (n_core * n_x)
    core_half = jax.ShapeDtypeStruct((n_x, width, block_cols), BF16)
    mine, other = pl.pallas_call(
        functools.partial(term_kernel, keep),
        out_shape=(core_half, core_half),
        in_specs=[SMEM, SMEM, VMEM, VMEM, VMEM, VMEM],
        out_specs=(VMEM, VMEM),
        scratch_shapes=[pltpu.VMEM((rows, width), BF16)],
        compiler_params=PARAMS,
        cost_estimate=cost(0, 8 * width),
        name="term",
    )(lax.axis_index("core").reshape(1), own_lengths, uvqk, grad_out, seg_col, seg_row)
    part = added(mine, permuted(other, "core", lambda i: i ^ 1)).astype(BF16)
    part = scatter_sum(part, "x")
    own_rows = width // n_z
    part, block = lax.optimization_barrier((part, block[source_of]))
    block = exchange(block)
    part = ring_of_rings_sum(part.reshape(n_z, own_rows, block_cols), "z", min(4, n_z)).astype(BF16)
    part = lax.optimization_barrier((part, block))[0]
    part = exchange(jnp.broadcast_to(part[None], (n_y,) + part.shape), "y")
    grad_rows = pl.pallas_call(
        functools.partial(back_kernel, keep),
        out_shape=jax.ShapeDtypeStruct(uvqk.shape, BF16),
        in_specs=[SMEM] + [VMEM] * 6,
        out_specs=VMEM,
        scratch_shapes=[pltpu.VMEM((moved, 5 * width), BF16)],
        compiler_params=PARAMS,
        cost_estimate=cost(8 * rows * width * width, 8 * width * width),
        name="back",
    )(recv_lengths, uvqk, grad_out, block, w_all, seg_col, seg_row)
    part, grad_rows = lax.optimization_barrier((part, grad_rows))
    part = (jnp.sum(part.astype(F32), axis=0) * (1.0 / (groups * n_z))).astype(BF16)
    spread = exchange(jnp.broadcast_to(part[None], (n_x * n_core,) + part.shape), ("x", "core"))
    spread = spread.reshape(n_x, n_core, own_rows, block_cols).transpose(2, 1, 0, 3)
    grad_weight = spread.reshape(own_rows, width).astype(F32)
    return grad_rows, grad_weight


def fine_mesh(mesh):
    n_dp, n_z = mesh.devices.shape
    n_core = 2
    n_x = min(4, n_dp // 4)
    shape = (n_x, n_dp // (n_x * n_core), n_core, n_z)
    return Mesh(mesh.devices.reshape(shape), ("x", "y", "core", "z"))


def solution(mesh):
    everyone = P(("x", "y", "core", "z"), None)
    placed = (everyone, everyone, P("z", None), everyone, P(), P())
    return jax.shard_map(
        local,
        mesh=fine_mesh(mesh),
        in_specs=placed,
        out_specs=(everyone, P("z", None)),
        check_vma=False,
    )
```

```python
import functools
import math

import jax
import jax.numpy as jnp
from jax import lax
from jax.experimental import pallas as pl
from jax.experimental.pallas import tpu as pltpu
from jax.sharding import Mesh
from jax.sharding import PartitionSpec as P

HEADS = 4
EPS = 1e-05
GROUP_ROWS = 16
BF16 = jnp.bfloat16
F32 = jnp.float32
DP = ("x", "y", "core")


def dot(a, b, dims):
    return lax.dot_general(a, b, (dims, ((), ())), preferred_element_type=F32)


def segments_of(ends, shape, dim):
    places = lax.broadcasted_iota(jnp.int32, shape, dim)
    passed = jnp.zeros(shape, jnp.int32)
    for end in ends:
        passed = passed + (places >= end).astype(jnp.int32)
    return jnp.where(passed == len(ends), -1, passed)


def masks(seg_column, seg_row):
    length = seg_column.shape[0]
    square = (length, length)
    same = seg_column == seg_row
    earlier = lax.broadcasted_iota(jnp.int32, square, 1) <= lax.broadcasted_iota(jnp.int32, square, 0)
    allowed = same & earlier & (seg_column >= 0)
    counts = jnp.sum(same.astype(F32), axis=1, keepdims=True)
    return allowed, counts


def forward(values, queries, key_rows, allowed, counts):
    width = values.shape[1]
    head_dim = width // HEADS
    scale = 1.0 / math.sqrt(head_dim)
    scores, sigmas, weights, mixed = [], [], [], []
    for h in range(HEADS):
        cols = slice(h * head_dim, (h + 1) * head_dim)
        s = dot(queries[:, cols], key_rows[:, cols], ((1,), (1,))) * scale
        sigma = jax.nn.sigmoid(s)
        w = (jnp.where(allowed, s * sigma, 0.0) / counts).astype(BF16)
        scores.append(s)
        sigmas.append(sigma)
        weights.append(w)
        mixed.append(dot(w, values[:, cols], ((1,), (0,))))
    mixed = jnp.concatenate(mixed, axis=1)
    centered = mixed - jnp.mean(mixed, axis=1, keepdims=True)
    inverse = lax.rsqrt(jnp.mean(centered * centered, axis=1, keepdims=True) + EPS)
    return scores, sigmas, weights, centered * inverse, inverse


def backward(gate, values, queries, key_rows, grad_y, allowed, counts, put):
    width = values.shape[1]
    head_dim = width // HEADS
    scale = 1.0 / math.sqrt(head_dim)
    scores, sigmas, weights, normed, inverse = forward(values, queries, key_rows, allowed, counts)
    put(0, slice(0, width), grad_y * normed)
    grad_normed = grad_y * gate.astype(F32)
    grad_mixed = inverse * (
        grad_normed
        - jnp.mean(grad_normed, axis=1, keepdims=True)
        - normed * jnp.mean(grad_normed * normed, axis=1, keepdims=True)
    )
    grad_mixed = grad_mixed.astype(BF16)
    factor = scale / counts
    for h in range(HEADS):
        cols = slice(h * head_dim, (h + 1) * head_dim)
        s, sigma = scores[h], sigmas[h]
        grad_weights = dot(grad_mixed[:, cols], values[:, cols], ((1,), (1,)))
        put(1, cols, dot(weights[h], grad_mixed[:, cols], ((0,), (0,))))
        slope = sigma * (1.0 + s * (1.0 - sigma))
        grad_scores = (jnp.where(allowed, grad_weights * slope, 0.0) * factor).astype(BF16)
        put(2, cols, dot(grad_scores, key_rows[:, cols], ((1,), (0,))))
        put(3, cols, dot(grad_scores, queries[:, cols], ((0,), (0,))))


def shares(row_groups, col_groups, share_cols):
    for r in range(row_groups):
        for c in range(col_groups):
            yield r * col_groups + c, r * GROUP_ROWS, c * share_cols


def pack_kernel(keep, x_ref, g_ref, out_ref, block_ref, sems):
    width, joint = x_ref.shape[1], block_ref.shape[1]
    moved = block_ref.shape[0]
    share_cols = out_ref.shape[2]
    rows = pl.ds(keep, moved)
    from_x = pltpu.make_async_copy(x_ref.at[rows], block_ref.at[:, pl.ds(0, width)], sems.at[0])
    from_g = pltpu.make_async_copy(g_ref.at[rows], block_ref.at[:, pl.ds(width, joint - width)], sems.at[1])
    from_x.start()
    from_g.start()
    from_x.wait()
    from_g.wait()
    for share, row, start in shares(moved // GROUP_ROWS, joint // share_cols, share_cols):
        out_ref[share] = block_ref[pl.ds(row, GROUP_ROWS), pl.ds(start, share_cols)]


def term_kernel(keep, core_ref, lengths_ref, x_ref, g_ref, seg_col_ref, seg_row_ref, mine_ref, other_ref, y_ref):
    width = g_ref.shape[1]
    rows_all = x_ref.shape[0]

    def rows_of(rows, allowed, counts):
        values, queries, key_rows = (x_ref[rows, pl.ds((1 + i) * width, width)] for i in range(3))
        normed = forward(values, queries, key_rows, allowed, counts)[3]
        y_ref[rows, :] = (normed * x_ref[rows, pl.ds(0, width)].astype(F32)).astype(BF16)

    moved = rows_all - keep
    total, ends = 0, []
    for i in range(lengths_ref.shape[1]):
        total = total + lengths_ref[0, i]
        ends.append(total)
    rows_of(pl.ds(keep, moved), *masks(segments_of(ends, (moved, 1), 0), segments_of(ends, (1, moved), 1)))
    rows_of(pl.ds(0, keep), *masks(seg_col_ref[...], seg_row_ref[...]))
    blocks, _, block_cols = mine_ref.shape
    joined = max(1, 256 // block_cols)
    core = core_ref[0]
    for half, term_ref in ((core, mine_ref), (1 - core, other_ref)):
        for b in range(0, blocks, joined):
            start = pl.multiple_of((half * blocks + b) * block_cols, 128)
            found = dot(g_ref[...], y_ref[:, pl.ds(start, joined * block_cols)], ((0,), (0,)))
            for i in range(joined):
                term_ref[b + i] = found[:, i * block_cols : (i + 1) * block_cols].astype(BF16)


def back_kernel(keep, lengths_ref, x_ref, g_ref, came_ref, w_ref, seg_col_ref, seg_row_ref, out_ref, block_ref):
    width = g_ref.shape[1]
    moved, joint = block_ref.shape
    share_cols = came_ref.shape[2]
    for share, row, start in shares(moved // GROUP_ROWS, joint // share_cols, share_cols):
        block_ref[pl.ds(row, GROUP_ROWS), pl.ds(start, share_cols)] = came_ref[share]

    def put_in(rows):
        def put(part, cols, found):
            out_ref[rows, pl.ds(part * width + cols.start, cols.stop - cols.start)] = found.astype(BF16)

        return put

    total, ends = 0, []
    for i in range(lengths_ref.shape[1]):
        total = total + lengths_ref[0, i]
        ends.append(total)
    kept_grad_y = dot(g_ref[pl.ds(0, keep), :], w_ref[...], ((1,), (0,)))
    parts = [x_ref[pl.ds(0, keep), pl.ds(i * width, width)] for i in range(4)]
    backward(*parts, kept_grad_y, *masks(seg_col_ref[...], seg_row_ref[...]), put_in(pl.ds(0, keep)))
    *parts, grads = [block_ref[:, pl.ds(i * width, width)] for i in range(5)]
    grad_y = dot(grads, w_ref[...], ((1,), (0,)))
    backward(
        *parts,
        grad_y,
        *masks(segments_of(ends, (moved, 1), 0), segments_of(ends, (1, moved), 1)),
        put_in(pl.ds(keep, moved)),
    )


VMEM = pl.BlockSpec(memory_space=pltpu.VMEM)
HBM = pl.BlockSpec(memory_space=pltpu.HBM)
SMEM = pl.BlockSpec(memory_space=pltpu.SMEM)
PARAMS = pltpu.CompilerParams(vmem_limit_bytes=24 * 2**20)


def cost(flops, nbytes):
    return pl.CostEstimate(flops=flops, bytes_accessed=nbytes, transcendentals=0)


def permuted(value, axis, target):
    size = lax.axis_size(axis)
    return lax.ppermute(value, axis, [(i, target(i)) for i in range(size)])


def pick(value, index, dim=0):
    return lax.dynamic_index_in_dim(value, index, dim, keepdims=False)


def added(*values):
    return functools.reduce(jnp.add, [value.astype(F32) for value in values])


def scatter_sum(value, axis, beside):
    size, me = lax.axis_size(axis), lax.axis_index(axis)
    came = [
        permuted(pick(value, (me + step) & (size - 1)), axis, lambda i, step=step: (i + step) % size)
        for step in range(1, size)
    ]
    came, beside = lax.optimization_barrier((came, beside))
    return added(pick(value, me), *came).astype(BF16), beside


def ring_of_rings_sum(value, axis, inner):
    size, me = lax.axis_size(axis), lax.axis_index(axis)
    outer = size // inner
    value = value.reshape((outer, inner) + value.shape[1:])
    low, high = me & (inner - 1), me >> (inner.bit_length() - 1)
    came = [
        permuted(
            pick(value, (low + step) & (inner - 1), 1),
            axis,
            lambda i, step=step: i // inner * inner + (i + step) % inner,
        )
        for step in range(1, inner)
    ]
    value = added(pick(value, low, 1), *came).astype(BF16)
    came = [
        permuted(pick(value, (high + step) & (outer - 1)), axis, lambda i, step=step: (i + step * inner) % size)
        for step in range(1, outer)
    ]
    return added(pick(value, high), *came)


def exchange(value, axes=DP):
    return lax.all_to_all(value, axes, split_axis=0, concat_axis=0, tiled=True)


def local(uvqk, grad_out, w_out, kept_segments, moved_lengths, dest_device):
    keep = kept_segments.shape[1]
    rows, width = grad_out.shape
    moved = rows - keep
    n_x, n_y, n_core, n_z = (lax.axis_size(a) for a in ("x", "y", "core", "z"))
    groups = n_x * n_y * n_core
    dp_index, z_index = lax.axis_index(DP), lax.axis_index("z")
    indices = jnp.arange(groups, dtype=jnp.int32)
    seg_col, seg_row = kept_segments.reshape(keep, 1), kept_segments

    w_all = lax.all_gather(w_out, "z", axis=0, tiled=True)
    share_cols = 5 * width * (moved // GROUP_ROWS) // groups
    block = pl.pallas_call(
        functools.partial(pack_kernel, keep),
        out_shape=jax.ShapeDtypeStruct((groups, GROUP_ROWS, share_cols), BF16),
        in_specs=[HBM, HBM],
        out_specs=VMEM,
        scratch_shapes=[pltpu.VMEM((moved, 5 * width), BF16), pltpu.SemaphoreType.DMA((2,))],
        compiler_params=pltpu.CompilerParams(vmem_limit_bytes=60 * 2**20),
        cost_estimate=cost(0, 8 * width),
        name="pack",
    )(uvqk, grad_out)
    uvqk, grad_out, dest_device, block = lax.optimization_barrier((uvqk, grad_out, dest_device, block))
    block = exchange(block)

    source_of = jnp.sum(jnp.where(dest_device[None, :] == indices[:, None], indices[None, :], 0), axis=1)
    own_source = jnp.sum(jnp.where(dest_device == dp_index, indices, 0))
    own_lengths = lax.dynamic_slice_in_dim(moved_lengths, dp_index * n_z + z_index, 1, 0)
    recv_lengths = lax.dynamic_slice_in_dim(moved_lengths, own_source * n_z + z_index, 1, 0)
    block_cols = width // (n_core * n_x)
    core_half = jax.ShapeDtypeStruct((n_x, width, block_cols), BF16)
    mine, other = pl.pallas_call(
        functools.partial(term_kernel, keep),
        out_shape=(core_half, core_half),
        in_specs=[SMEM, SMEM, VMEM, VMEM, VMEM, VMEM],
        out_specs=(VMEM, VMEM),
        scratch_shapes=[pltpu.VMEM((rows, width), BF16)],
        compiler_params=PARAMS,
        cost_estimate=cost(0, 8 * width),
        name="term",
    )(lax.axis_index("core").reshape(1), own_lengths, uvqk, grad_out, seg_col, seg_row)
    part = added(mine, permuted(other, "core", lambda i: i ^ 1)).astype(BF16)
    part, block = scatter_sum(part, "x", block[source_of])
    own_rows = width // n_z
    part, block = lax.optimization_barrier((part, block))
    block = exchange(block)
    part = ring_of_rings_sum(part.reshape(n_z, own_rows, block_cols), "z", min(4, n_z)).astype(BF16)
    part = lax.optimization_barrier((part, block))[0]
    part = exchange(jnp.broadcast_to(part[None], (n_y,) + part.shape), "y")
    grad_rows = pl.pallas_call(
        functools.partial(back_kernel, keep),
        out_shape=jax.ShapeDtypeStruct(uvqk.shape, BF16),
        in_specs=[SMEM] + [VMEM] * 6,
        out_specs=VMEM,
        scratch_shapes=[pltpu.VMEM((moved, 5 * width), BF16)],
        compiler_params=PARAMS,
        cost_estimate=cost(8 * rows * width * width, 8 * width * width),
        name="back",
    )(recv_lengths, uvqk, grad_out, block, w_all, seg_col, seg_row)
    part, grad_rows = lax.optimization_barrier((part, grad_rows))
    part = (jnp.sum(part.astype(F32), axis=0) * (1.0 / (groups * n_z))).astype(BF16)
    spread = exchange(jnp.broadcast_to(part[None], (n_x * n_core,) + part.shape), ("x", "core"))
    spread = spread.reshape(n_x, n_core, own_rows, block_cols).transpose(2, 1, 0, 3)
    grad_weight = spread.reshape(own_rows, width).astype(F32)
    return grad_rows, grad_weight


def fine_mesh(mesh):
    n_dp, n_z = mesh.devices.shape
    n_core = 2
    n_x = min(4, n_dp // 4)
    shape = (n_x, n_dp // (n_x * n_core), n_core, n_z)
    return Mesh(mesh.devices.reshape(shape), ("x", "y", "core", "z"))


def solution(mesh):
    everyone = P(("x", "y", "core", "z"), None)
    placed = (everyone, everyone, P("z", None), everyone, P(), P())
    return jax.shard_map(
        local,
        mesh=fine_mesh(mesh),
        in_specs=placed,
        out_specs=(everyone, P("z", None)),
        check_vma=False,
    )
```
